256 devices in a mesh: slide: 16 (over x, y_hi, core), rep: 16 (over z, y_lo).
Axes of the slice: x: 4, y: 4 (y_hi: 2, y_lo: 2; y = y_hi * 2 + y_lo), z: 8, core: 2. Of those that a mesh axis runs over, the one named last changes fastest.
Arguments:
- tile_images: bfloat16 [1024, 32, 32, 384], P(('slide', 'rep')), may hold values from -6 to 6
- cotangent: bfloat16 [1024, 32, 32, 384], P(('slide', 'rep')), may hold values from -0.1875 to 0.1875
- depth_kernel: bfloat16 [7, 7, 384], replicated, may hold values from -0.875 to 0.875
- depth_bias: float32 [384], replicated, may hold values from -3 to 3
- norm_gain: float32 [384], replicated, may hold values from 0.5 to 2
- norm_bias: float32 [384], replicated, may hold values from -3 to 3
- expand_weight: bfloat16 [1536, 384], replicated, may hold values from -0.3125 to 0.3125
- expand_bias: float32 [1536], replicated, may hold values from -3 to 3
- project_weight: bfloat16 [1536, 384], replicated, may hold values from -0.15625 to 0.15625
- layer_scale: float32 [384], replicated, may hold values from 0.1 to 1
- tile_counts: int32 [16, 16], P('slide', 'rep'), may hold values from 1 to 4, as said below
- send_list: int32 [16, 16, 16], P('slide', 'rep'), may hold values from -1 to 31, as said below
Outputs:
- grad_expand: float32 [1536, 384], P(('slide', 'rep'))
- grad_project: float32 [1536, 384], P(('slide', 'rep'))
The draws below stay inside these ranges and needn't reach their ends.
Inputs may be any that keep to these rules, and one draw needn't show every extreme that they name: Every device holds its tiles in its first tile_counts slots; some device holds 4 tiles and some device one. `send_list`: the blocks that a device names are distinct and lie in its first tile_counts tiles; each device names at least one block and at most 16, at most one for each destination, and some device names 16; each device (d, r) is named as destination by at most 5 devices, and some device by exactly 5.
All inputs are finite; a program needn't handle non-finite values.
Results may differ from the reference program's by a relative error of at most 0.0055.
Values may be sent and summed in bfloat16 or wider, within the bound.
No kernel may reach another device: no remote copies, remote signals or barrier semaphores. Data moves between devices by JAX's collectives and lax.ppermute only.
A program may use at most 128 MiB of HBM per device.

```python
import math
import jax
import jax.numpy as jnp
from jax import lax

D = 384
HID = 1536
KS = 7
SIDE = 32
RECV_MOST = 5
BAND_ROWS = 4
TILES_DEV = 4
SHARDS = 16
REPS = 16
BANDS = 8
BAND_TOK = 128
TILES = 1024


def make_plan(key):
    total = SHARDS * REPS
    bands = SIDE // BAND_ROWS
    blocks = TILES_DEV * bands
    keys = jax.random.split(jax.random.fold_in(key, 7), 6)
    position = jnp.arange(total, dtype=jnp.int32)
    slide_of = position // REPS
    rep_of = position % REPS
    counts = jax.random.randint(keys[0], (total,), 1, TILES_DEV + 1).astype(jnp.int32)
    top_dev = jax.random.randint(keys[1], (), 0, total).astype(jnp.int32)
    low_dev = ((top_dev + 1 + jax.random.randint(keys[2], (), 0, total - 1)) % total).astype(jnp.int32)
    counts = jnp.where(position == top_dev, TILES_DEV, jnp.where(position == low_dev, 1, counts)).astype(jnp.int32)
    top_slide = top_dev // REPS
    top_rep = top_dev % REPS
    dest_index = jnp.arange(SHARDS, dtype=jnp.int32)
    shift_scores = jax.random.randint(keys[3], (REPS, SHARDS), 0, 2 ** 20) * SHARDS + dest_index[None, :]
    offsets = jnp.argsort(shift_scores.astype(jnp.int32), axis=1, stable=True).astype(jnp.int32)
    device_offsets = offsets[rep_of]
    favoured = (top_slide + offsets[top_rep, RECV_MOST - 1]) % SHARDS
    sends = jnp.zeros((total, SHARDS), dtype=bool)
    for layer in range(RECV_MOST - 1):
        target = (slide_of + device_offsets[:, layer]) % SHARDS
        if layer == 0:
            active = jnp.ones((total,), dtype=bool)
        else:
            coin = jax.random.randint(jax.random.fold_in(keys[4], layer), (total,), 0, 2) == 1
            forced = (rep_of == top_rep) & (target == favoured)
            active = coin | forced
        sends = sends | (dest_index[None, :] == target[:, None]) & active[:, None]
    sends = sends | (position == top_dev)[:, None]
    block_index = jnp.arange(blocks, dtype=jnp.int32)
    scores = jax.random.randint(keys[5], (total, blocks), 0, 2 ** 20) * blocks + block_index[None, :]
    scores = jnp.where(block_index[None, :] >= (counts * bands)[:, None], scores + 2 ** 30, scores)
    forced_block = (position[:, None] == top_dev) & (block_index[None, :] == blocks - 1)
    scores = jnp.where(forced_block, -1, scores).astype(jnp.int32)
    block_order = jnp.argsort(scores, axis=1, stable=True).astype(jnp.int32)
    chosen = block_order[:, :SHARDS]
    rank = (jnp.cumsum(sends.astype(jnp.int32), axis=1) - 1).astype(jnp.int32)
    rank = jnp.clip(rank, 0, SHARDS - 1).astype(jnp.int32)
    named = jnp.take_along_axis(chosen, rank, axis=1)
    send_rows = jnp.where(sends, named, -1).astype(jnp.int32)
    return (counts.reshape(SHARDS, REPS), send_rows.reshape(SHARDS, REPS, SHARDS))


def draw_tile_counts(key, part):
    return make_plan(key)[0]


def draw_send_list(key, part):
    return make_plan(key)[1]


def shard_levels(stream_key, dims, shards, low, largest):
    def one(dim, shards_of):
        steps = jax.random.uniform(jax.random.fold_in(jax.random.fold_in(stream_key, 6), dim), (shards_of,), jnp.float32, low / len(shards), largest / len(shards))
        return jnp.repeat(jnp.exp(steps), dims[dim] // shards_of).reshape((-1,) + (1,) * (len(dims) - dim - 1))

    loudness = one(*shards[0])
    for cut in shards[1:]:
        loudness = loudness * one(*cut)
    return loudness


def noise(rng, shape, deviation, limit, cuts=(), kind=jnp.bfloat16):
    array = jax.random.normal(rng, shape, jnp.float32) * deviation
    if len(cuts) > 0:
        array = shard_levels(rng, shape, cuts, -0.22, 0.18) * array
    return jnp.clip(array, min=-limit, max=limit).astype(kind)


def setup_inputs(seed: int = 0) -> dict:
    key_of = jax.random.split(jax.random.key(seed), 13)
    tile_images = noise(key_of[0], (TILES, SIDE, SIDE, D), 1.0, 6.0, ((0, 256),))
    cotangent = noise(key_of[1], (TILES, SIDE, SIDE, D), (1 / SIDE), 0.1875, ((0, 256),))
    depth_kernel = noise(key_of[2], (KS, KS, D), (KS * KS) ** -0.5, 0.875)
    depth_bias = noise(key_of[3], (D,), 0.5, 3.0, (), jnp.float32)
    norm_gain = jnp.clip(jnp.exp(jax.random.uniform(key_of[4], (D,), jnp.float32, math.log(0.5), math.log(2.0))), 0.5, 2.0)
    norm_bias = noise(key_of[5], (D,), 0.5, 3.0, (), jnp.float32)
    expand_weight = noise(key_of[6], (HID, D), D ** -0.5, 0.3125)
    expand_bias = noise(key_of[7], (HID,), 0.5, 3.0, (), jnp.float32)
    project_weight = noise(key_of[8], (HID, D), HID ** -0.5, 0.15625)
    layer_scale = jnp.clip(jnp.exp(jax.random.uniform(key_of[9], (D,), jnp.float32, math.log(0.1), math.log(1.0))), 0.1, 1.0)
    tile_counts = draw_tile_counts(jax.random.fold_in(key_of[12], 71), 0)
    send_list = draw_send_list(jax.random.fold_in(key_of[12], 71), 0)
    return dict(tile_images=tile_images, cotangent=cotangent, depth_kernel=depth_kernel, depth_bias=depth_bias, norm_gain=norm_gain, norm_bias=norm_bias, expand_weight=expand_weight, expand_bias=expand_bias, project_weight=project_weight, layer_scale=layer_scale, tile_counts=tile_counts, send_list=send_list)


root_half = 0.7071067811865476
inv_root_tau = 0.3989422804014327

def gelu_value(pre_act):
    return 0.5 * pre_act * (1.0 + lax.erf(pre_act * root_half))

def gelu_slope(pre_act):
    return 0.5 * (1.0 + lax.erf(pre_act * root_half)) + pre_act * jnp.exp(-0.5 * pre_act * pre_act) * inv_root_tau

def to_blocks(field):
    return field.reshape(field.shape[0] * BANDS, BAND_TOK, field.shape[-1])

def prepare(images_one, cotan_one, held_count, depth_kernel, depth_bias, norm_gain, norm_bias, layer_scale):
    channels = images_one.shape[-1]
    kernel = depth_kernel.reshape(KS, KS, 1, channels)
    margin = KS // 2
    mixed_conv = lax.conv_general_dilated(images_one, kernel, (1, 1), ((margin, margin), (margin, margin)), dimension_numbers=('NHWC', 'HWIO', 'NHWC'), feature_group_count=channels, preferred_element_type=jnp.float32)
    mixed_conv = mixed_conv + depth_bias
    centre = lax.optimization_barrier(jnp.mean(mixed_conv, axis=-1, keepdims=True))
    spread = lax.optimization_barrier(jnp.mean(jnp.square(mixed_conv - centre), axis=-1, keepdims=True))
    normed = ((mixed_conv - centre) * lax.rsqrt(spread + 1e-06) * norm_gain + norm_bias).astype(jnp.bfloat16)
    scaled = (cotan_one.astype(jnp.float32) * (layer_scale / held_count.astype(jnp.float32))).astype(jnp.bfloat16)
    return (to_blocks(normed), to_blocks(scaled))

def contribute(totals, piece_in, piece_err, expand_weight, expand_bias, project_weight):
    pre_act = jnp.dot(piece_in, expand_weight.T, preferred_element_type=jnp.float32) + expand_bias
    activated = gelu_value(pre_act).astype(jnp.bfloat16)
    back_grad = jnp.dot(piece_err, project_weight.T, preferred_element_type=jnp.float32)
    slope_term = (back_grad * gelu_slope(pre_act)).astype(jnp.bfloat16)
    grad_in = totals[0] + jnp.dot(slope_term.T, piece_in, preferred_element_type=jnp.float32)
    grad_out = totals[1] + jnp.dot(activated.T, piece_err, preferred_element_type=jnp.float32)
    return (grad_in, grad_out)

def reference(tile_images, cotangent, depth_kernel, depth_bias, norm_gain, norm_bias, expand_weight, expand_bias, project_weight, layer_scale, tile_counts, send_list):
    device_total = SHARDS * REPS
    images = tile_images.reshape(device_total, TILES_DEV, SIDE, SIDE, D)
    cotans = cotangent.reshape(device_total, TILES_DEV, SIDE, SIDE, D)
    held_all = tile_counts.reshape(device_total)
    send_rows = send_list.reshape(device_total, SHARDS)
    empty_grad = jnp.zeros((HID, D), jnp.float32)

    def per_device(totals, operands):
        images_one, cotan_one, held_count, slot_ids = operands
        normed, scaled = prepare(images_one, cotan_one, held_count, depth_kernel, depth_bias, norm_gain, norm_bias, layer_scale)

        def per_slot(partial_sums, slot_id):

            def include(running):
                chosen = jnp.maximum(slot_id, 0)
                return contribute(running, normed[chosen], scaled[chosen], expand_weight, expand_bias, project_weight)

            def skipped(running):
                return running
            return (lax.cond(slot_id >= 0, include, skipped, partial_sums), None)
        totals, _ = lax.scan(per_slot, totals, slot_ids)
        return (totals, None)
    totals, _ = lax.scan(per_device, (empty_grad, empty_grad), (images, cotans, held_all, send_rows))
    return (totals[0], totals[1])
```

```python
import functools

import jax
import jax.numpy as jnp
from jax import lax
from jax.experimental import pallas as pl
from jax.experimental.pallas import tpu as pltpu
from jax.sharding import PartitionSpec as P

BANDS = 8
BAND_ROWS = 4
BAND_TOK = 128
SLOTS = 16
GROUP = 2
HID_STEP = 512

root_half = 0.7071067811865476
inv_root_tau = 0.3989422804014327

INNER = (((1,), (1,)), ((), ()))
PLAIN = (((1,), (0,)), ((), ()))


def local_kernel(
    slots_ref,
    count_ref,
    core_ref,
    images_hbm,
    cotan_hbm,
    taps_ref,
    depth_bias_ref,
    gain_ref,
    norm_bias_ref,
    scale_ref,
    expand_ref,
    expand_bias_ref,
    project_ref,
    keep_ref,
    send_ref,
    padded,
    cotans,
    normed,
    scaled,
    conv_out,
    grad_in,
    grad_out,
    order_ref,
    sems,
):
    tiles, side, _, channels = images_hbm.shape
    margin = 3
    hidden = expand_ref.shape[0]
    held = count_ref[0]

    def image_copy(tile):
        return pltpu.make_async_copy(
            images_hbm.at[tile], padded.at[tile, pl.ds(margin, side)], sems.at[0, tile]
        )

    def cotan_copy(tile):
        return pltpu.make_async_copy(cotan_hbm.at[tile], cotans.at[tile], sems.at[1, tile])

    for tile in range(tiles):
        image_copy(tile).start()
    for tile in range(tiles):
        cotan_copy(tile).start()

    listed = jnp.int32(0)
    for slot in range(SLOTS):
        block = slots_ref[slot]
        order_ref[listed] = jnp.maximum(block, 0)
        listed = listed + jnp.where(block >= 0, 1, 0)

    for tile in range(tiles):
        padded[tile, :margin] = jnp.zeros((margin, side, channels), padded.dtype)
        padded[tile, margin + side :] = jnp.zeros((margin, side, channels), padded.dtype)
    grad_in[...] = jnp.zeros(grad_in.shape, jnp.float32)
    grad_out[...] = jnp.zeros(grad_out.shape, jnp.float32)

    for tile in range(tiles):
        image_copy(tile).wait()
    for tile in range(tiles):
        cotan_copy(tile).wait()

    scale = scale_ref[...] / held.astype(jnp.float32)
    column = lax.broadcasted_iota(jnp.int32, (side, 128), 0)
    inside = {
        dx: (column + dx >= 0) & (column + dx < side) for dx in range(-margin, margin + 1)
    }

    @pl.loop(0, listed)
    def _(index):
        block = order_ref[index]
        tile = block // BANDS
        first = (block % BANDS) * BAND_ROWS
        for lanes in range(0, channels, 128):
            part = pl.ds(lanes, 128)
            for row in range(BAND_ROWS):
                sums = [None] * 7
                for dy in range(7):
                    x = padded[tile, first + (row + dy), :, part].astype(jnp.float32)
                    for dx in range(7):
                        term = x * taps_ref[dy * 7 + dx : dy * 7 + dx + 1, part]
                        sums[dx] = term if sums[dx] is None else sums[dx] + term
                total = sums[margin] + depth_bias_ref[:, part]
                for dx in range(-margin, margin + 1):
                    if dx != 0:
                        moved = pltpu.roll(sums[dx + margin], (-dx) % side, 0)
                        total = total + jnp.where(inside[dx], moved, 0.0)
                conv_out[row * side : (row + 1) * side, part] = total
        mixed = conv_out[...]
        centre = jnp.mean(mixed, axis=-1, keepdims=True)
        away = mixed - centre
        spread = jnp.mean(away * away, axis=-1, keepdims=True)
        rows = pl.ds(pl.multiple_of(index * BAND_TOK, BAND_TOK), BAND_TOK)
        normed[rows, :] = (
            away * lax.rsqrt(spread + 1e-06) * gain_ref[...] + norm_bias_ref[...]
        ).astype(normed.dtype)
        err = cotans[tile, pl.ds(first, BAND_ROWS)].reshape(BAND_TOK, channels)
        scaled[rows, :] = (err.astype(jnp.float32) * scale).astype(scaled.dtype)

    @pl.when(listed % GROUP != 0)
    def _():
        rows = pl.ds(pl.multiple_of(listed * BAND_TOK, BAND_TOK), BAND_TOK)
        normed[rows, :] = jnp.zeros((BAND_TOK, channels), normed.dtype)
        scaled[rows, :] = jnp.zeros((BAND_TOK, channels), scaled.dtype)

    span = GROUP * BAND_TOK

    @pl.loop(0, (listed + GROUP - 1) // GROUP)
    def _(group):
        rows = pl.ds(pl.multiple_of(group * span, span), span)
        flat_in = normed[rows, :]
        flat_err = scaled[rows, :]
        for start in range(0, hidden, HID_STEP):
            units = pl.ds(start, HID_STEP)
            pre_act = lax.dot_general(
                expand_ref[units, :], flat_in, INNER, preferred_element_type=jnp.float32
            )
            back_grad = lax.dot_general(
                project_ref[units, :], flat_err, INNER, preferred_element_type=jnp.float32
            )
            pre_act = pre_act + expand_bias_ref[units, :]
            share = 0.5 * (1.0 + lax.erf(pre_act * root_half))
            activated = (pre_act * share).astype(jnp.bfloat16)
            bell = jnp.exp(-0.5 * pre_act * pre_act) * inv_root_tau
            slope_term = (back_grad * (share + pre_act * bell)).astype(jnp.bfloat16)
            grad_in[units, :] += lax.dot_general(
                slope_term, flat_in, PLAIN, preferred_element_type=jnp.float32
            )
            grad_out[units, :] += lax.dot_general(
                activated, flat_err, PLAIN, preferred_element_type=jnp.float32
            )

    core = core_ref[0]
    rows = hidden // SLOTS
    for pair in range(SLOTS // 2):
        mine = pl.ds(pl.multiple_of((2 * pair + core) * rows, rows), rows)
        other = pl.ds(pl.multiple_of((2 * pair + 1 - core) * rows, rows), rows)
        for which, grad in enumerate((grad_in, grad_out)):
            keep_ref[which, pair] = grad[mine, :]
            send_ref[which, pair] = grad[other, :].astype(send_ref.dtype)


def local_grads(
    slots,
    count,
    core,
    tile_images,
    cotangent,
    depth_kernel,
    depth_bias,
    norm_gain,
    norm_bias,
    expand_weight,
    expand_bias,
    project_weight,
    layer_scale,
):
    tiles, side, _, channels = tile_images.shape
    hidden = expand_weight.shape[0]
    rows = hidden // SLOTS
    row = lambda v: v.reshape(1, -1)
    smem = pl.BlockSpec(memory_space=pltpu.SMEM)
    vmem = pl.BlockSpec(memory_space=pltpu.VMEM)
    hbm = pl.BlockSpec(memory_space=pl.ANY)
    return pl.pallas_call(
        local_kernel,
        out_shape=(
            jax.ShapeDtypeStruct((2, SLOTS // 2, rows, channels), jnp.float32),
            jax.ShapeDtypeStruct((2, SLOTS // 2, rows, channels), jnp.bfloat16),
        ),
        in_specs=[smem] * 3 + [hbm] * 2 + [vmem] * 8,
        out_specs=[vmem] * 2,
        scratch_shapes=[
            pltpu.VMEM((tiles, side + 6, side, channels), jnp.bfloat16),
            pltpu.VMEM((tiles, side, side, channels), jnp.bfloat16),
            pltpu.VMEM((SLOTS * BAND_TOK, channels), jnp.bfloat16),
            pltpu.VMEM((SLOTS * BAND_TOK, channels), jnp.bfloat16),
            pltpu.VMEM((BAND_TOK, channels), jnp.float32),
            pltpu.VMEM((hidden, channels), jnp.float32),
            pltpu.VMEM((hidden, channels), jnp.float32),
            pltpu.SMEM((SLOTS + 1,), jnp.int32),
            pltpu.SemaphoreType.DMA((2, tiles)),
        ],
        compiler_params=pltpu.CompilerParams(vmem_limit_bytes=56 * 2**20),
        name="local_grads",
    )(
        slots,
        count,
        core,
        tile_images,
        cotangent,
        depth_kernel.reshape(-1, channels).astype(jnp.float32),
        row(depth_bias),
        row(norm_gain),
        row(norm_bias),
        row(layer_scale),
        expand_weight,
        expand_bias.reshape(-1, 1),
        project_weight,
    )


def spread_sum(total, axis_index, axis_size, link, target):
    own = lax.dynamic_index_in_dim(total, axis_index, 0, keepdims=False)
    got = []
    for step in range(1, axis_size):
        away = lax.dynamic_index_in_dim(
            total, lax.rem(axis_index + step, axis_size), 0, keepdims=False
        )
        got.append(target(away.astype(link), step))
    for piece in got:
        own = own + piece.astype(jnp.float32)
    return own


def reduce_all(keep, send):
    channels = keep.shape[-1]
    slide, rep = lax.axis_index("slide"), lax.axis_index("rep")
    from_core = lax.ppermute(send, "slide", [(i, i ^ 1) for i in range(16)])
    total = keep + from_core.astype(jnp.float32)
    total = total.reshape(2, 4, 2, -1, channels).transpose(1, 0, 2, 3, 4)
    total = spread_sum(
        total,
        slide // 4,
        4,
        jnp.bfloat16,
        lambda a, k: lax.ppermute(a, "slide", [(i, (i + 4 * k) % 16) for i in range(16)]),
    )
    total = total.reshape(2, 2, 8, 2, -1, channels).transpose(1, 3, 0, 2, 4, 5)
    total = total.reshape((4,) + total.shape[2:])
    place = (slide // 2) % 2 * 2 + rep % 2

    def along_y(a, k):
        pairs = []
        for s in range(16):
            for r in range(16):
                y = (s // 2) % 2 * 2 + r % 2
                to = (y + k) % 4
                pairs.append((s * 16 + r, ((s & ~2) | (to // 2 * 2)) * 16 + ((r & ~1) | to % 2)))
        return lax.ppermute(a, ("slide", "rep"), pairs)

    total = spread_sum(total, place, 4, jnp.bfloat16, along_y)
    total = total.transpose(1, 0, 2, 3)
    total = spread_sum(
        total,
        rep // 2,
        8,
        jnp.float32,
        lambda a, k: lax.ppermute(a, "rep", [(i, (i + 2 * k) % 16) for i in range(16)]),
    )
    return total[0], total[1]


def per_device(
    tile_images,
    cotangent,
    depth_kernel,
    depth_bias,
    norm_gain,
    norm_bias,
    expand_weight,
    expand_bias,
    project_weight,
    layer_scale,
    tile_counts,
    send_list,
):
    core = lax.rem(lax.axis_index("slide"), 2).astype(jnp.int32)
    keep, send = local_grads(
        send_list.reshape(-1),
        tile_counts.reshape(-1),
        core.reshape(1),
        tile_images,
        cotangent,
        depth_kernel,
        depth_bias,
        norm_gain,
        norm_bias,
        expand_weight,
        expand_bias,
        project_weight,
        layer_scale,
    )
    return reduce_all(keep, send)


def solution(mesh):
    in_specs = (
        P(("slide", "rep"), None, None, None),
        P(("slide", "rep"), None, None, None),
        P(),
        P(),
        P(),
        P(),
        P(),
        P(),
        P(),
        P(),
        P("slide", "rep"),
        P("slide", "rep", None),
    )
    out_specs = (P(("slide", "rep"), None), P(("slide", "rep"), None))
    return jax.shard_map(
        per_device, mesh=mesh, in_specs=in_specs, out_specs=out_specs, check_vma=False
    )
```

```python
import jax
import jax.numpy as jnp
from jax import lax
from jax.experimental import pallas as pl
from jax.experimental.pallas import tpu as pltpu
from jax.sharding import PartitionSpec as P

BANDS = 8
BAND_ROWS = 4
BAND_TOK = 128
SLOTS = 16
GROUP = 2
SPAN = GROUP * BAND_TOK
GROUPS = SLOTS // GROUP
PAIRS = 8
CHUNK = 96
PART = 48
SHARE = 6
MARGIN = 3

root_half = 0.7071067811865476
inv_root_tau = 0.3989422804014327

INNER = (((1,), (1,)), ((), ()))
PLAIN = (((1,), (0,)), ((), ()))


def half_copies(weight_hbm, weight, which_half, sems):
    copies = []
    for pair in range(PAIRS):
        first = pl.multiple_of((2 * pair + which_half) * CHUNK, CHUNK)
        copies.append(
            pltpu.make_async_copy(
                weight_hbm.at[pl.ds(first, CHUNK)],
                weight.at[pl.ds(pair * CHUNK, CHUNK)],
                sems.at[pair],
            )
        )
    return copies


def add_group(group, normed, scaled, expand, project, bias, grad_in, grad_out):
    rows = pl.ds(pl.multiple_of(group * SPAN, SPAN), SPAN)
    flat_in = normed[rows, :]
    flat_err = scaled[rows, :]
    pre_act = lax.dot_general(expand[...], flat_in, INNER, preferred_element_type=jnp.float32)
    back_grad = lax.dot_general(project[...], flat_err, INNER, preferred_element_type=jnp.float32)
    column = bias[...]
    pre_act = pre_act + jnp.concatenate([column] * (SPAN // 128), axis=1)
    share = 0.5 * (1.0 + lax.erf(pre_act * root_half))
    activated = (pre_act * share).astype(jnp.bfloat16)
    bell = jnp.exp(-0.5 * pre_act * pre_act) * inv_root_tau
    slope_term = (back_grad * (share + pre_act * bell)).astype(jnp.bfloat16)
    grad_in[...] += lax.dot_general(slope_term, flat_in, PLAIN, preferred_element_type=jnp.float32)
    grad_out[...] += lax.dot_general(activated, flat_err, PLAIN, preferred_element_type=jnp.float32)


def count_listed(slots_ref):
    listed = jnp.int32(0)
    for slot in range(SLOTS):
        listed = listed + jnp.where(slots_ref[slot] >= 0, 1, 0)
    return listed


def first_kernel(
    slots_ref,
    count_ref,
    core_ref,
    images_hbm,
    cotan_hbm,
    taps_ref,
    depth_bias_ref,
    gain_ref,
    norm_bias_ref,
    scale_ref,
    expand_hbm,
    expand_bias_ref,
    project_hbm,
    acts_hbm,
    bias_ref,
    send_ref,
    images,
    cotans,
    taps,
    normed,
    scaled,
    conv_out,
    bias_all,
    bias_other,
    expand,
    project,
    grad_in,
    grad_out,
    order_ref,
    image_sems,
    cotan_sems,
    weight_sems,
    acts_sems,
):
    side = images_hbm.shape[1]
    channels = images_hbm.shape[3]
    core = core_ref[0]

    listed = jnp.int32(0)
    for slot in range(SLOTS):
        block = slots_ref[slot]
        order_ref[listed] = jnp.maximum(block, 0)
        listed = listed + jnp.where(block >= 0, 1, 0)

    def copies(index):
        block = order_ref[index]
        tile = block // BANDS
        band = block % BANDS
        first = band * BAND_ROWS
        above = pltpu.make_async_copy(
            images_hbm.at[tile, pl.ds(first - MARGIN, MARGIN)],
            images.at[index, pl.ds(0, MARGIN)],
            image_sems.at[index, 0],
        )
        middle = pltpu.make_async_copy(
            images_hbm.at[tile, pl.ds(first, BAND_ROWS)],
            images.at[index, pl.ds(MARGIN, BAND_ROWS)],
            image_sems.at[index, 1],
        )
        below = pltpu.make_async_copy(
            images_hbm.at[tile, pl.ds(first + BAND_ROWS, MARGIN)],
            images.at[index, pl.ds(MARGIN + BAND_ROWS, MARGIN)],
            image_sems.at[index, 2],
        )
        error = pltpu.make_async_copy(
            cotan_hbm.at[tile, pl.ds(first, BAND_ROWS)],
            cotans.at[index],
            cotan_sems.at[index],
        )
        return band > 0, band < BANDS - 1, above, middle, below, error

    @pl.loop(0, listed)
    def _(index):
        has_above, has_below, above, middle, below, error = copies(index)
        pl.when(has_above)(above.start)
        middle.start()
        pl.when(has_below)(below.start)
        error.start()

    weight_copies = half_copies(expand_hbm, expand, 1 - core, weight_sems.at[0])
    weight_copies += half_copies(project_hbm, project, 1 - core, weight_sems.at[1])
    for copy in weight_copies:
        copy.start()

    taps[...] = taps_ref[...].astype(jnp.float32)
    hidden = expand_bias_ref.shape[0]
    for first in range(0, hidden, 128):
        row = expand_bias_ref[pl.ds(first, 128)].reshape(1, 128)
        bias_all[pl.ds(first, 128), :] = jnp.broadcast_to(row, (128, 128)).T
    for pair in range(PAIRS):
        mine = pl.ds(pl.multiple_of((2 * pair + core) * CHUNK, CHUNK), CHUNK)
        other = pl.ds(pl.multiple_of((2 * pair + 1 - core) * CHUNK, CHUNK), CHUNK)
        bias_ref[pl.ds(pair * CHUNK, CHUNK), :] = bias_all[mine, :]
        bias_other[pl.ds(pair * CHUNK, CHUNK), :] = bias_all[other, :]
    grad_in[...] = jnp.zeros(grad_in.shape, jnp.float32)
    grad_out[...] = jnp.zeros(grad_out.shape, jnp.float32)

    depth_bias = depth_bias_ref[...].reshape(1, channels)
    gain = gain_ref[...].reshape(1, channels)
    norm_bias = norm_bias_ref[...].reshape(1, channels)
    scale = scale_ref[...].reshape(1, channels) / count_ref[0].astype(jnp.float32)
    column = lax.broadcasted_iota(jnp.int32, (side, 128), 0)
    inside = {
        dx: (column + dx >= 0) & (column + dx < side) for dx in range(-MARGIN, MARGIN + 1)
    }

    @pl.loop(0, listed)
    def _(index):
        has_above, has_below, above, middle, below, error = copies(index)

        @pl.when(has_above)
        def _():
            above.wait()

        @pl.when(jnp.logical_not(has_above))
        def _():
            images[index, :MARGIN] = jnp.zeros((MARGIN, side, channels), images.dtype)

        @pl.when(has_below)
        def _():
            below.wait()

        @pl.when(jnp.logical_not(has_below))
        def _():
            images[index, MARGIN + BAND_ROWS :] = jnp.zeros(
                (MARGIN, side, channels), images.dtype
            )

        middle.wait()
        for lanes in range(0, channels, 128):
            part = slice(lanes, lanes + 128)
            for row in range(BAND_ROWS):
                sums = [None] * 7
                for dy in range(7):
                    x = images[index, row + dy, :, part].astype(jnp.float32)
                    for dx in range(7):
                        term = x * taps[dy, dx : dx + 1, part]
                        sums[dx] = term if sums[dx] is None else sums[dx] + term
                total = sums[MARGIN] + depth_bias[:, part]
                for dx in range(-MARGIN, MARGIN + 1):
                    if dx != 0:
                        moved = pltpu.roll(sums[dx + MARGIN], (-dx) % side, 0)
                        total = total + jnp.where(inside[dx], moved, 0.0)
                conv_out[row * side : (row + 1) * side, part] = total
        mixed = conv_out[...]
        centre = jnp.mean(mixed, axis=-1, keepdims=True)
        away = mixed - centre
        spread = jnp.mean(away * away, axis=-1, keepdims=True)
        rows = pl.ds(pl.multiple_of(index * BAND_TOK, BAND_TOK), BAND_TOK)
        normed[rows, :] = (away * lax.rsqrt(spread + 1e-06) * gain + norm_bias).astype(
            normed.dtype
        )
        error.wait()
        err = cotans[index].reshape(BAND_TOK, channels)
        scaled[rows, :] = (err.astype(jnp.float32) * scale).astype(scaled.dtype)

    @pl.when(listed % GROUP != 0)
    def _():
        rows = pl.ds(pl.multiple_of(listed * BAND_TOK, BAND_TOK), BAND_TOK)
        normed[rows, :] = jnp.zeros((BAND_TOK, channels), normed.dtype)
        scaled[rows, :] = jnp.zeros((BAND_TOK, channels), scaled.dtype)

    groups = (listed + GROUP - 1) // GROUP

    def acts_copies(group):
        rows = pl.ds(pl.multiple_of(group * SPAN, SPAN), SPAN)
        return [
            pltpu.make_async_copy(acts.at[rows], acts_hbm.at[which, rows], acts_sems.at[which, group])
            for which, acts in enumerate((normed, scaled))
        ]

    for copy in weight_copies:
        copy.wait()

    @pl.loop(0, groups)
    def _(group):
        for copy in acts_copies(group):
            copy.start()
        add_group(group, normed, scaled, expand, project, bias_other, grad_in, grad_out)

    send_ref[0] = grad_in[...].astype(send_ref.dtype)
    send_ref[1] = grad_out[...].astype(send_ref.dtype)

    @pl.loop(0, groups)
    def _(group):
        for copy in acts_copies(group):
            copy.wait()


def second_kernel(
    slots_ref,
    core_ref,
    acts_hbm,
    bias_ref,
    expand_hbm,
    project_hbm,
    keep_ref,
    normed,
    scaled,
    expand,
    project,
    weight_sems,
    acts_sems,
):
    core = core_ref[0]
    groups = (count_listed(slots_ref) + GROUP - 1) // GROUP
    weight_copies = half_copies(expand_hbm, expand, core, weight_sems.at[0])
    weight_copies += half_copies(project_hbm, project, core, weight_sems.at[1])

    def acts_copies(group):
        rows = pl.ds(pl.multiple_of(group * SPAN, SPAN), SPAN)
        return [
            pltpu.make_async_copy(acts_hbm.at[which, rows], acts.at[rows], acts_sems.at[which, group])
            for which, acts in enumerate((normed, scaled))
        ]

    for copy in weight_copies:
        copy.start()

    @pl.loop(0, groups)
    def _(group):
        for copy in acts_copies(group):
            copy.start()

    keep_ref[...] = jnp.zeros(keep_ref.shape, jnp.float32)
    for copy in weight_copies:
        copy.wait()

    @pl.loop(0, groups)
    def _(group):
        for copy in acts_copies(group):
            copy.wait()
        add_group(
            group, normed, scaled, expand, project, bias_ref, keep_ref.at[0], keep_ref.at[1]
        )


SMEM = pl.BlockSpec(memory_space=pltpu.SMEM)
VMEM = pl.BlockSpec(memory_space=pltpu.VMEM)
HBM = pl.BlockSpec(memory_space=pl.ANY)


def params(mib):
    return pltpu.CompilerParams(vmem_limit_bytes=mib * 2**20)


def local_first(
    slots,
    count,
    core,
    tile_images,
    cotangent,
    depth_kernel,
    depth_bias,
    norm_gain,
    norm_bias,
    expand_weight,
    expand_bias,
    project_weight,
    layer_scale,
):
    side, channels = tile_images.shape[1], tile_images.shape[3]
    hidden = expand_weight.shape[0]
    half = hidden // 2
    bf16, f32 = jnp.bfloat16, jnp.float32
    return pl.pallas_call(
        first_kernel,
        out_shape=(
            jax.ShapeDtypeStruct((2, SLOTS * BAND_TOK, channels), bf16),
            jax.ShapeDtypeStruct((half, 128), f32),
            jax.ShapeDtypeStruct((2, half, channels), bf16),
        ),
        in_specs=[SMEM] * 3 + [HBM] * 2 + [VMEM] * 5 + [HBM, VMEM, HBM],
        out_specs=[HBM, VMEM, VMEM],
        scratch_shapes=[
            pltpu.VMEM((SLOTS, BAND_ROWS + 2 * MARGIN, side, channels), bf16),
            pltpu.VMEM((SLOTS, BAND_ROWS, side, channels), bf16),
            pltpu.VMEM((7, 7, channels), f32),
            pltpu.VMEM((SLOTS * BAND_TOK, channels), bf16),
            pltpu.VMEM((SLOTS * BAND_TOK, channels), bf16),
            pltpu.VMEM((BAND_TOK, channels), f32),
            pltpu.VMEM((hidden, 128), f32),
            pltpu.VMEM((half, 128), f32),
            pltpu.VMEM((half, channels), bf16),
            pltpu.VMEM((half, channels), bf16),
            pltpu.VMEM((half, channels), f32),
            pltpu.VMEM((half, channels), f32),
            pltpu.SMEM((SLOTS + 1,), jnp.int32),
            pltpu.SemaphoreType.DMA((SLOTS, 3)),
            pltpu.SemaphoreType.DMA((SLOTS,)),
            pltpu.SemaphoreType.DMA((2, PAIRS)),
            pltpu.SemaphoreType.DMA((2, GROUPS)),
        ],
        compiler_params=params(26),
        cost_estimate=pl.CostEstimate(flops=8 * 10**9, bytes_accessed=10**7, transcendentals=0),
        name="conv_and_other_half",
    )(
        slots,
        count,
        core,
        tile_images,
        cotangent,
        depth_kernel,
        depth_bias,
        norm_gain,
        norm_bias,
        layer_scale,
        expand_weight,
        expand_bias,
        project_weight,
    )


def local_second(slots, core, acts, bias, expand_weight, project_weight):
    hidden, channels = expand_weight.shape
    half = hidden // 2
    bf16, f32 = jnp.bfloat16, jnp.float32
    return pl.pallas_call(
        second_kernel,
        out_shape=jax.ShapeDtypeStruct((2, half, channels), f32),
        in_specs=[SMEM] * 2 + [HBM, VMEM, HBM, HBM],
        out_specs=VMEM,
        scratch_shapes=[
            pltpu.VMEM((SLOTS * BAND_TOK, channels), bf16),
            pltpu.VMEM((SLOTS * BAND_TOK, channels), bf16),
            pltpu.VMEM((half, channels), bf16),
            pltpu.VMEM((half, channels), bf16),
            pltpu.SemaphoreType.DMA((2, PAIRS)),
            pltpu.SemaphoreType.DMA((2, GROUPS)),
        ],
        compiler_params=params(16),
        cost_estimate=pl.CostEstimate(flops=5 * 10**9, bytes_accessed=6 * 10**6, transcendentals=0),
        name="own_half",
    )(slots, core, acts, bias, expand_weight, project_weight)


def arrange_kernel(place_ref, keep_ref, got_ref, *refs):
    in_keep, in_send, out_keep, out_send = refs[0], refs[1:4], refs[4], refs[5:8]
    sums = refs[8]
    new = lax.broadcasted_iota(jnp.int32, (CHUNK, CHUNK), 0)
    old = lax.broadcasted_iota(jnp.int32, (CHUNK, CHUNK), 1)
    share = (new * 43) >> 8
    source = ((share & 7) * 2 + (share >> 3)) * SHARE + (new - share * SHARE)
    move = jnp.where(old == source, 1.0, 0.0).astype(jnp.bfloat16)
    for which in range(2):
        for pair in range(PAIRS):
            rows = slice(pair * CHUNK, (pair + 1) * CHUNK)
            total = keep_ref[which, rows, :] + got_ref[which, rows, :].astype(jnp.float32)
            high = total.astype(jnp.bfloat16)
            low = (total - high.astype(jnp.float32)).astype(jnp.bfloat16)
            moved = lax.dot_general(
                move, high, PLAIN, preferred_element_type=jnp.float32
            ) + lax.dot_general(move, low, PLAIN, preferred_element_type=jnp.float32)
            x, y_high = pair // 2, pair % 2
            for y_low in range(2):
                piece = moved[y_low * PART : (y_low + 1) * PART]
                if which == 0:
                    sums[0, x, 2 * y_high + y_low] = piece
                else:
                    sums[1, 2 * y_high + y_low, x] = piece
    for which, keep, send in ((0, in_keep, in_send), (1, out_keep, out_send)):
        here = place_ref[which]
        keep[...] = sums[which, here]
        for step in range(1, 4):
            there = (here + step) & 3
            send[step - 1][...] = sums[which, there].astype(jnp.bfloat16)


def arrange(place, keep, got):
    channels = keep.shape[-1]
    own = jax.ShapeDtypeStruct((4, PART, channels), jnp.float32)
    away = jax.ShapeDtypeStruct((4, PART, channels), jnp.bfloat16)
    return pl.pallas_call(
        arrange_kernel,
        out_shape=[own, away, away, away, own, away, away, away],
        in_specs=[SMEM, VMEM, VMEM],
        out_specs=[VMEM] * 8,
        scratch_shapes=[pltpu.VMEM((2, 4, 4, PART, channels), jnp.float32)],
        compiler_params=params(14),
        name="arrange",
    )(place, keep, got)


def middle_kernel(place_ref, *refs):
    ins, outs, sums = refs[:8], refs[8:16], refs[16]
    for which in range(2):
        keep, got = ins[4 * which], ins[4 * which + 1 : 4 * which + 4]
        total = keep[...]
        for piece in got:
            total = total + piece[...].astype(jnp.float32)
        sums[which] = total
        here = place_ref[1 - which]
        outs[4 * which][...] = sums[which, here]
        for step in range(1, 4):
            there = (here + step) & 3
            outs[4 * which + step][...] = sums[which, there].astype(jnp.bfloat16)


def middle(place, *ins):
    channels = ins[0].shape[-1]
    own = jax.ShapeDtypeStruct((PART, channels), jnp.float32)
    away = jax.ShapeDtypeStruct((PART, channels), jnp.bfloat16)
    return pl.pallas_call(
        middle_kernel,
        out_shape=[own, away, away, away] * 2,
        in_specs=[SMEM] + [VMEM] * 8,
        out_specs=[VMEM] * 8,
        scratch_shapes=[pltpu.VMEM((2, 4, PART, channels), jnp.float32)],
        compiler_params=params(6),
        name="middle",
    )(place, *ins)


def last_kernel(place_ref, *refs):
    ins, outs, sums = refs[:8], refs[8:16], refs[16]
    for which in range(2):
        total = ins[4 * which][...]
        for piece in ins[4 * which + 1 : 4 * which + 4]:
            total = total + piece[...].astype(jnp.float32)
        for z in range(8):
            sums[z, which] = total[z * SHARE : (z + 1) * SHARE]
    here = place_ref[2]
    for step in range(8):
        outs[step][...] = sums[(here + step) & 7]


def last(place, *ins):
    channels = ins[0].shape[-1]
    piece = jax.ShapeDtypeStruct((2, SHARE, channels), jnp.float32)
    return pl.pallas_call(
        last_kernel,
        out_shape=[piece] * 8,
        in_specs=[SMEM] + [VMEM] * 8,
        out_specs=[VMEM] * 8,
        scratch_shapes=[pltpu.VMEM((8, 2, SHARE, channels), jnp.float32)],
        compiler_params=params(4),
        name="last",
    )(place, *ins)


def along_x(a, step):
    return lax.ppermute(a, "slide", [(i, (i + 4 * step) % 16) for i in range(16)])


def along_y(a, step):
    pairs = []
    for s in range(16):
        for r in range(16):
            to = ((s // 2) % 2 * 2 + r % 2 + step) % 4
            pairs.append((s * 16 + r, ((s & ~2) | (to // 2 * 2)) * 16 + ((r & ~1) | to % 2)))
    return lax.ppermute(a, ("slide", "rep"), pairs)


def along_z(a, step):
    return lax.ppermute(a, "rep", [(i, (i + 2 * step) % 16) for i in range(16)])


def per_device(
    tile_images,
    cotangent,
    depth_kernel,
    depth_bias,
    norm_gain,
    norm_bias,
    expand_weight,
    expand_bias,
    project_weight,
    layer_scale,
    tile_counts,
    send_list,
):
    slide, rep = lax.axis_index("slide"), lax.axis_index("rep")
    place = jnp.stack([slide // 4, (slide // 2) % 2 * 2 + rep % 2, rep // 2]).astype(jnp.int32)
    core = lax.rem(slide, 2).astype(jnp.int32).reshape(1)
    slots = send_list.reshape(-1)
    acts, bias, send = local_first(
        slots,
        tile_counts.reshape(-1),
        core,
        tile_images,
        cotangent,
        depth_kernel,
        depth_bias,
        norm_gain,
        norm_bias,
        expand_weight,
        expand_bias,
        project_weight,
        layer_scale,
    )
    got = lax.ppermute(send, "slide", [(i, i ^ 1) for i in range(16)])
    keep = local_second(slots, core, acts, bias, expand_weight, project_weight)
    pieces = arrange(place, keep, got)
    pieces = (
        [pieces[0]]
        + [along_x(pieces[step], step) for step in range(1, 4)]
        + [pieces[4]]
        + [along_y(pieces[4 + step], step) for step in range(1, 4)]
    )
    pieces = middle(place, *pieces)
    pieces = (
        [pieces[0]]
        + [along_y(pieces[step], step) for step in range(1, 4)]
        + [pieces[4]]
        + [along_x(pieces[4 + step], step) for step in range(1, 4)]
    )
    pieces = last(place, *pieces)
    total = pieces[0]
    for step in range(1, 8):
        total = total + along_z(pieces[step], step)
    return total[0], total[1]


def solution(mesh):
    in_specs = (
        P(("slide", "rep"), None, None, None),
        P(("slide", "rep"), None, None, None),
        P(),
        P(),
        P(),
        P(),
        P(),
        P(),
        P(),
        P(),
        P("slide", "rep"),
        P("slide", "rep", None),
    )
    out_specs = (P(("slide", "rep"), None), P(("slide", "rep"), None))
    return jax.shard_map(
        per_device, mesh=mesh, in_specs=in_specs, out_specs=out_specs, check_vma=False
    )
```

```python
import jax
import jax.numpy as jnp
from jax import lax
from jax.experimental import pallas as pl
from jax.experimental.pallas import tpu as pltpu
from jax.sharding import PartitionSpec as P

BANDS = 8
MARGIN = 3
BAND_ROWS = 4
BAND_TOK = 128
SLOTS = 16
GROUP = 2
KEPT = 8
ROWS = BAND_ROWS + 2 * MARGIN
HID_STEP = 768
SPAN = GROUP * BAND_TOK
GROUPS = SLOTS // GROUP
PAIRS = 8
CHUNK = 96
PART = 48
SHARE = 6

root_half = 0.7071067811865476
inv_root_tau = 0.3989422804014327

INNER = (((1,), (1,)), ((), ()))
PLAIN = (((1,), (0,)), ((), ()))


def half_copies(weight_hbm, weight, core, sems):
    copies = []
    for half in range(2):
        for pair in range(PAIRS):
            first = pl.multiple_of((2 * pair + (core ^ half)) * CHUNK, CHUNK)
            copies.append(
                pltpu.make_async_copy(
                    weight_hbm.at[pl.ds(first, CHUNK)],
                    weight.at[pl.ds((half * PAIRS + pair) * CHUNK, CHUNK)],
                    sems.at[half, pair],
                )
            )
    return copies


def pack_list(slots_ref, order_ref):
    listed = jnp.int32(0)
    for slot in range(SLOTS):
        block = slots_ref[slot]
        order_ref[listed] = jnp.maximum(block, 0)
        listed = listed + jnp.where(block >= 0, 1, 0)
    return listed


def moved_count(listed, listed_there):
    surplus = jnp.maximum(listed - listed_there - 1, 0) >> 1
    return jnp.minimum(surplus, jnp.maximum(listed - KEPT, 0))


def block_copies(order_ref, index, images_hbm, cotan_hbm, images, cotans, sems):
    block = order_ref[index]
    tile = block // BANDS
    band = block % BANDS
    first = band * BAND_ROWS
    above = pltpu.make_async_copy(
        images_hbm.at[tile, pl.ds(first - MARGIN, MARGIN)], images.at[pl.ds(0, MARGIN)], sems.at[0]
    )
    middle = pltpu.make_async_copy(
        images_hbm.at[tile, pl.ds(first, BAND_ROWS)], images.at[pl.ds(MARGIN, BAND_ROWS)], sems.at[1]
    )
    below = pltpu.make_async_copy(
        images_hbm.at[tile, pl.ds(first + BAND_ROWS, MARGIN)],
        images.at[pl.ds(MARGIN + BAND_ROWS, MARGIN)],
        sems.at[2],
    )
    error = pltpu.make_async_copy(cotan_hbm.at[tile, pl.ds(first, BAND_ROWS)], cotans, sems.at[3])
    return band, above, middle, below, error


def start_block(band, above, middle, below, error):
    pl.when(band > 0)(above.start)
    middle.start()
    pl.when(band < BANDS - 1)(below.start)
    error.start()


def pack_kernel(slots_ref, images_hbm, cotan_hbm, packed_hbm, order_ref, sems):
    listed = pack_list(slots_ref, order_ref)

    def copies(index):
        place = packed_hbm.at[index - KEPT]
        return block_copies(
            order_ref,
            index,
            images_hbm,
            cotan_hbm,
            place.at[pl.ds(0, ROWS)],
            place.at[pl.ds(ROWS, BAND_ROWS)],
            sems.at[index],
        )

    @pl.loop(KEPT, listed)
    def _(index):
        start_block(*copies(index))

    @pl.loop(KEPT, listed)
    def _(index):
        band, above, middle, below, error = copies(index)
        pl.when(band > 0)(above.wait)
        middle.wait()
        pl.when(band < BANDS - 1)(below.wait)
        error.wait()


def conv_norm(image, band, taps, conv_out, depth_bias, gain, norm_bias):
    _, side, channels = image.shape

    @pl.when(band == 0)
    def _():
        image[:MARGIN] = jnp.zeros((MARGIN, side, channels), image.dtype)

    @pl.when(band == BANDS - 1)
    def _():
        image[MARGIN + BAND_ROWS : ROWS] = jnp.zeros((MARGIN, side, channels), image.dtype)

    column = lax.broadcasted_iota(jnp.int32, (side, 128), 0)
    for lanes in range(0, channels, 128):
        part = slice(lanes, lanes + 128)
        for row in range(BAND_ROWS):
            sums = [None] * 7
            for dy in range(7):
                x = image[row + dy, :, part].astype(jnp.float32)
                for dx in range(7):
                    term = x * taps[dy, dx : dx + 1, part]
                    sums[dx] = term if sums[dx] is None else sums[dx] + term
            total = sums[MARGIN] + depth_bias[:, part]
            for dx in range(-MARGIN, MARGIN + 1):
                if dx != 0:
                    moved = pltpu.roll(sums[dx + MARGIN], (-dx) % side, 0)
                    inside = (column + dx >= 0) & (column + dx < side)
                    total = total + jnp.where(inside, moved, 0.0)
            conv_out[row * side : (row + 1) * side, part] = total
    mixed = conv_out[...]
    centre = jnp.mean(mixed, axis=-1, keepdims=True)
    away = mixed - centre
    spread = jnp.mean(away * away, axis=-1, keepdims=True)
    return (away * lax.rsqrt(spread + 1e-06) * gain + norm_bias).astype(jnp.bfloat16)


def scale_errors(errors, scale):
    rows, side, channels = errors.shape
    flat = errors[...].reshape(rows * side, channels)
    return (flat.astype(jnp.float32) * scale).astype(jnp.bfloat16)


def conv_kernel(
    slots_ref,
    there_ref,
    count_ref,
    core_ref,
    images_hbm,
    cotan_hbm,
    taps_ref,
    depth_bias_ref,
    gain_ref,
    norm_bias_ref,
    scale_ref,
    expand_bias_ref,
    acts_hbm,
    bias_ref,
    images,
    cotans,
    taps,
    acts,
    conv_out,
    bias_all,
    order_ref,
    image_sems,
    acts_sems,
):
    channels = images_hbm.shape[3]
    core = core_ref[0]
    listed = pack_list(slots_ref, order_ref)
    listed_there = jnp.int32(0)
    for slot in range(SLOTS):
        listed_there = listed_there + jnp.where(there_ref[slot] >= 0, 1, 0)
    own = listed - moved_count(listed, listed_there)

    def copies(index):
        return block_copies(
            order_ref,
            index,
            images_hbm,
            cotan_hbm,
            images.at[index],
            cotans.at[index],
            image_sems.at[index],
        )

    @pl.loop(0, own)
    def _(index):
        start_block(*copies(index))

    taps[...] = taps_ref[...].astype(jnp.float32)
    hidden = expand_bias_ref.shape[0]
    for first in range(0, hidden, 128):
        row = expand_bias_ref[pl.ds(first, 128)].reshape(1, 128)
        bias_all[pl.ds(first, 128), :] = jnp.broadcast_to(row, (128, 128)).T
    for half in range(2):
        for pair in range(PAIRS):
            rows = pl.ds(pl.multiple_of((2 * pair + (core ^ half)) * CHUNK, CHUNK), CHUNK)
            bias_ref[pl.ds((half * PAIRS + pair) * CHUNK, CHUNK), :] = bias_all[rows, :]

    depth_bias = depth_bias_ref[...].reshape(1, channels)
    gain = gain_ref[...].reshape(1, channels)
    norm_bias = norm_bias_ref[...].reshape(1, channels)
    scale = scale_ref[...].reshape(1, channels) / count_ref[0].astype(jnp.float32)

    def acts_copy(index):
        rows = pl.ds(pl.multiple_of(index * BAND_TOK, BAND_TOK), BAND_TOK)
        return pltpu.make_async_copy(acts.at[:, rows], acts_hbm.at[:, rows], acts_sems.at[index])

    @pl.loop(0, own)
    def _(index):
        band, above, middle, below, error = copies(index)
        pl.when(band > 0)(above.wait)
        middle.wait()
        pl.when(band < BANDS - 1)(below.wait)
        rows = pl.ds(pl.multiple_of(index * BAND_TOK, BAND_TOK), BAND_TOK)
        acts[0, rows, :] = conv_norm(
            images.at[index], band, taps, conv_out, depth_bias, gain, norm_bias
        )
        error.wait()
        acts[1, rows, :] = scale_errors(cotans.at[index], scale)
        acts_copy(index).start()

    @pl.loop(0, own)
    def _(index):
        acts_copy(index).wait()


def train_kernel(
    slots_ref,
    there_ref,
    count_there_ref,
    core_ref,
    acts_hbm,
    packed_hbm,
    taps_ref,
    depth_bias_ref,
    gain_ref,
    norm_bias_ref,
    scale_ref,
    expand_hbm,
    bias_ref,
    project_hbm,
    keep_ref,
    send_ref,
    packed,
    taps,
    acts,
    conv_out,
    expand,
    project,
    grad,
    order_ref,
    packed_sems,
    acts_sems,
    weight_sems,
):
    channels = packed_hbm.shape[3]
    core = core_ref[0]
    listed_there = pack_list(there_ref, order_ref)
    listed = jnp.int32(0)
    for slot in range(SLOTS):
        listed = listed + jnp.where(slots_ref[slot] >= 0, 1, 0)
    own = listed - moved_count(listed, listed_there)
    taken = moved_count(listed_there, listed)
    first_taken = listed_there - taken - KEPT

    def packed_copy(index):
        place = first_taken + index
        return pltpu.make_async_copy(packed_hbm.at[place], packed.at[place], packed_sems.at[place])

    def acts_copy(index):
        rows = pl.ds(pl.multiple_of(index * BAND_TOK, BAND_TOK), BAND_TOK)
        return pltpu.make_async_copy(acts_hbm.at[:, rows], acts.at[:, rows], acts_sems.at[index])

    @pl.loop(0, taken)
    def _(index):
        packed_copy(index).start()

    weight_copies = half_copies(expand_hbm, expand, core, weight_sems.at[0])
    weight_copies += half_copies(project_hbm, project, core, weight_sems.at[1])
    for copy in weight_copies:
        copy.start()

    @pl.loop(0, own)
    def _(index):
        acts_copy(index).start()

    taps[...] = taps_ref[...].astype(jnp.float32)
    depth_bias = depth_bias_ref[...].reshape(1, channels)
    gain = gain_ref[...].reshape(1, channels)
    norm_bias = norm_bias_ref[...].reshape(1, channels)
    scale = scale_ref[...].reshape(1, channels) / count_there_ref[0].astype(jnp.float32)
    keep_ref[...] = jnp.zeros(keep_ref.shape, jnp.float32)
    grad[...] = jnp.zeros(grad.shape, jnp.float32)

    @pl.loop(0, taken)
    def _(index):
        packed_copy(index).wait()
        place = first_taken + index
        rows = pl.ds(pl.multiple_of((own + index) * BAND_TOK, BAND_TOK), BAND_TOK)
        band = order_ref[KEPT + place] % BANDS
        acts[0, rows, :] = conv_norm(
            packed.at[place, pl.ds(0, ROWS)], band, taps, conv_out, depth_bias, gain, norm_bias
        )
        acts[1, rows, :] = scale_errors(packed.at[place, pl.ds(ROWS, BAND_ROWS)], scale)

    total = own + taken

    @pl.when(total % GROUP != 0)
    def _():
        rows = pl.ds(pl.multiple_of(total * BAND_TOK, BAND_TOK), BAND_TOK)
        acts[:, rows, :] = jnp.zeros((2, BAND_TOK, channels), acts.dtype)

    for copy in weight_copies:
        copy.wait()

    @pl.loop(0, own)
    def _(index):
        acts_copy(index).wait()

    half = keep_ref.shape[1]

    @pl.loop(0, (total + GROUP - 1) // GROUP)
    def _(group):
        rows = pl.ds(pl.multiple_of(group * SPAN, SPAN), SPAN)
        flat_in = acts[0, rows, :]
        flat_err = acts[1, rows, :]
        for start in range(0, 2 * half, HID_STEP):
            units = slice(start, start + HID_STEP)
            pre_act = lax.dot_general(
                expand[units, :], flat_in, INNER, preferred_element_type=jnp.float32
            )
            back_grad = lax.dot_general(
                project[units, :], flat_err, INNER, preferred_element_type=jnp.float32
            )
            pre_act = pre_act + jnp.concatenate([bias_ref[units, :]] * (SPAN // 128), axis=1)
            share = 0.5 * (1.0 + lax.erf(pre_act * root_half))
            activated = (pre_act * share).astype(jnp.bfloat16)
            bell = jnp.exp(-0.5 * pre_act * pre_act) * inv_root_tau
            slope_term = (back_grad * (share + pre_act * bell)).astype(jnp.bfloat16)
            sums, first = (keep_ref, start) if start < half else (grad, start - half)
            units = slice(first, first + HID_STEP)
            sums[0, units, :] += lax.dot_general(
                slope_term, flat_in, PLAIN, preferred_element_type=jnp.float32
            )
            sums[1, units, :] += lax.dot_general(
                activated, flat_err, PLAIN, preferred_element_type=jnp.float32
            )

    send_ref[...] = grad[...].astype(send_ref.dtype)


SMEM = pl.BlockSpec(memory_space=pltpu.SMEM)
VMEM = pl.BlockSpec(memory_space=pltpu.VMEM)
HBM = pl.BlockSpec(memory_space=pl.ANY)


def params(mib):
    return pltpu.CompilerParams(vmem_limit_bytes=mib * 2**20)


def pack(slots, tile_images, cotangent):
    side, channels = tile_images.shape[1], tile_images.shape[3]
    return pl.pallas_call(
        pack_kernel,
        out_shape=jax.ShapeDtypeStruct(
            (SLOTS - KEPT, ROWS + BAND_ROWS, side, channels), jnp.bfloat16
        ),
        in_specs=[SMEM, HBM, HBM],
        out_specs=HBM,
        scratch_shapes=[
            pltpu.SMEM((SLOTS + 1,), jnp.int32),
            pltpu.SemaphoreType.DMA((SLOTS, 4)),
        ],
        compiler_params=params(56),
        name="pack",
    )(slots, tile_images, cotangent)


def conv_own(slots, there, count, core, tile_images, cotangent, conv_weights, scale, expand_bias):
    side, channels = tile_images.shape[1], tile_images.shape[3]
    hidden = expand_bias.shape[0]
    bf16, f32 = jnp.bfloat16, jnp.float32
    return pl.pallas_call(
        conv_kernel,
        out_shape=(
            jax.ShapeDtypeStruct((2, SLOTS * BAND_TOK, channels), bf16),
            jax.ShapeDtypeStruct((hidden, 128), f32),
        ),
        in_specs=[SMEM] * 4 + [HBM] * 2 + [VMEM] * 6,
        out_specs=[HBM, VMEM],
        scratch_shapes=[
            pltpu.VMEM((SLOTS, ROWS, side, channels), bf16),
            pltpu.VMEM((SLOTS, BAND_ROWS, side, channels), bf16),
            pltpu.VMEM((7, 7, channels), f32),
            pltpu.VMEM((2, SLOTS * BAND_TOK, channels), bf16),
            pltpu.VMEM((BAND_TOK, channels), f32),
            pltpu.VMEM((hidden, 128), f32),
            pltpu.SMEM((SLOTS + 1,), jnp.int32),
            pltpu.SemaphoreType.DMA((SLOTS, 4)),
            pltpu.SemaphoreType.DMA((SLOTS,)),
        ],
        compiler_params=params(56),
        cost_estimate=pl.CostEstimate(flops=8 * 10**9, bytes_accessed=10**7, transcendentals=0),
        name="conv_own",
    )(slots, there, count, core, tile_images, cotangent, *conv_weights, scale, expand_bias)


def train(
    slots, there, count_there, core, acts, packed, conv_weights, scale, expand_weight, bias,
    project_weight,
):
    hidden, channels = expand_weight.shape
    half = hidden // 2
    bf16, f32 = jnp.bfloat16, jnp.float32
    return pl.pallas_call(
        train_kernel,
        out_shape=(
            jax.ShapeDtypeStruct((2, half, channels), f32),
            jax.ShapeDtypeStruct((2, half, channels), bf16),
        ),
        in_specs=[SMEM] * 4 + [HBM] * 2 + [VMEM] * 5 + [HBM, VMEM, HBM],
        out_specs=[VMEM, VMEM],
        scratch_shapes=[
            pltpu.VMEM(packed.shape, bf16),
            pltpu.VMEM((7, 7, channels), f32),
            pltpu.VMEM(acts.shape, bf16),
            pltpu.VMEM((BAND_TOK, channels), f32),
            pltpu.VMEM((hidden, channels), bf16),
            pltpu.VMEM((hidden, channels), bf16),
            pltpu.VMEM((2, half, channels), f32),
            pltpu.SMEM((SLOTS + 1,), jnp.int32),
            pltpu.SemaphoreType.DMA((SLOTS - KEPT,)),
            pltpu.SemaphoreType.DMA((SLOTS,)),
            pltpu.SemaphoreType.DMA((2, 2, PAIRS)),
        ],
        compiler_params=params(56),
        cost_estimate=pl.CostEstimate(flops=9 * 10**9, bytes_accessed=10**7, transcendentals=0),
        name="train",
    )(
        slots, there, count_there, core, acts, packed, *conv_weights, scale, expand_weight, bias,
        project_weight,
    )


def arrange_kernel(place_ref, keep_ref, got_ref, *refs):
    in_keep, in_send, out_keep, out_send = refs[0], refs[1:4], refs[4], refs[5:8]
    sums = refs[8]
    new = lax.broadcasted_iota(jnp.int32, (CHUNK, CHUNK), 0)
    old = lax.broadcasted_iota(jnp.int32, (CHUNK, CHUNK), 1)
    share = (new * 43) >> 8
    source = ((share & 7) * 2 + (share >> 3)) * SHARE + (new - share * SHARE)
    move = jnp.where(old == source, 1.0, 0.0).astype(jnp.bfloat16)
    for which in range(2):
        for pair in range(PAIRS):
            rows = slice(pair * CHUNK, (pair + 1) * CHUNK)
            total = keep_ref[which, rows, :] + got_ref[which, rows, :].astype(jnp.float32)
            high = total.astype(jnp.bfloat16)
            low = (total - high.astype(jnp.float32)).astype(jnp.bfloat16)
            moved = lax.dot_general(
                move, high, PLAIN, preferred_element_type=jnp.float32
            ) + lax.dot_general(move, low, PLAIN, preferred_element_type=jnp.float32)
            x, y_high = pair // 2, pair % 2
            for y_low in range(2):
                piece = moved[y_low * PART : (y_low + 1) * PART]
                if which == 0:
                    sums[0, x, 2 * y_high + y_low] = piece
                else:
                    sums[1, 2 * y_high + y_low, x] = piece
    for which, keep, send in ((0, in_keep, in_send), (1, out_keep, out_send)):
        here = place_ref[which]
        keep[...] = sums[which, here]
        for step in range(1, 4):
            there = (here + step) & 3
            send[step - 1][...] = sums[which, there].astype(jnp.bfloat16)


def arrange(place, keep, got):
    channels = keep.shape[-1]
    own = jax.ShapeDtypeStruct((4, PART, channels), jnp.float32)
    away = jax.ShapeDtypeStruct((4, PART, channels), jnp.bfloat16)
    return pl.pallas_call(
        arrange_kernel,
        out_shape=[own, away, away, away, own, away, away, away],
        in_specs=[SMEM, VMEM, VMEM],
        out_specs=[VMEM] * 8,
        scratch_shapes=[pltpu.VMEM((2, 4, 4, PART, channels), jnp.float32)],
        compiler_params=params(14),
        name="arrange",
    )(place, keep, got)


def middle_kernel(place_ref, *refs):
    ins, outs, sums = refs[:8], refs[8:16], refs[16]
    for which in range(2):
        keep, got = ins[4 * which], ins[4 * which + 1 : 4 * which + 4]
        total = keep[...]
        for piece in got:
            total = total + piece[...].astype(jnp.float32)
        sums[which] = total
        here = place_ref[1 - which]
        outs[4 * which][...] = sums[which, here]
        for step in range(1, 4):
            there = (here + step) & 3
            outs[4 * which + step][...] = sums[which, there].astype(jnp.bfloat16)


def middle(place, *ins):
    channels = ins[0].shape[-1]
    own = jax.ShapeDtypeStruct((PART, channels), jnp.float32)
    away = jax.ShapeDtypeStruct((PART, channels), jnp.bfloat16)
    return pl.pallas_call(
        middle_kernel,
        out_shape=[own, away, away, away] * 2,
        in_specs=[SMEM] + [VMEM] * 8,
        out_specs=[VMEM] * 8,
        scratch_shapes=[pltpu.VMEM((2, 4, PART, channels), jnp.float32)],
        compiler_params=params(6),
        name="middle",
    )(place, *ins)


def last_kernel(place_ref, *refs):
    ins, outs, sums = refs[:8], refs[8:16], refs[16]
    for which in range(2):
        total = ins[4 * which][...]
        for piece in ins[4 * which + 1 : 4 * which + 4]:
            total = total + piece[...].astype(jnp.float32)
        for z in range(8):
            sums[z, which] = total[z * SHARE : (z + 1) * SHARE]
    here = place_ref[2]
    for step in range(8):
        outs[step][...] = sums[(here + step) & 7]


def last(place, *ins):
    channels = ins[0].shape[-1]
    piece = jax.ShapeDtypeStruct((2, SHARE, channels), jnp.float32)
    return pl.pallas_call(
        last_kernel,
        out_shape=[piece] * 8,
        in_specs=[SMEM] + [VMEM] * 8,
        out_specs=[VMEM] * 8,
        scratch_shapes=[pltpu.VMEM((8, 2, SHARE, channels), jnp.float32)],
        compiler_params=params(4),
        name="last",
    )(place, *ins)


def along_x(a, step):
    return lax.ppermute(a, "slide", [(i, (i + 4 * step) % 16) for i in range(16)])


def along_y(a, step):
    pairs = []
    for s in range(16):
        for r in range(16):
            to = ((s // 2) % 2 * 2 + r % 2 + step) % 4
            pairs.append((s * 16 + r, ((s & ~2) | (to // 2 * 2)) * 16 + ((r & ~1) | to % 2)))
    return lax.ppermute(a, ("slide", "rep"), pairs)


def along_z(a, step):
    return lax.ppermute(a, "rep", [(i, (i + 2 * step) % 16) for i in range(16)])


def per_device(
    tile_images,
    cotangent,
    depth_kernel,
    depth_bias,
    norm_gain,
    norm_bias,
    expand_weight,
    expand_bias,
    project_weight,
    layer_scale,
    tile_counts,
    send_list,
):
    slide, rep = lax.axis_index("slide"), lax.axis_index("rep")
    place = jnp.stack([slide // 4, (slide // 2) % 2 * 2 + rep % 2, rep // 2]).astype(jnp.int32)
    core = lax.rem(slide, 2).astype(jnp.int32).reshape(1)
    slots = send_list.reshape(-1)
    count = tile_counts.reshape(-1)
    conv_weights = (depth_kernel, depth_bias, norm_gain, norm_bias)
    swap = [(i, i ^ 1) for i in range(16)]
    there = lax.ppermute(slots, "slide", swap)
    count_there = lax.ppermute(count, "slide", swap)
    packed = lax.ppermute(pack(slots, tile_images, cotangent), "slide", swap)
    acts, bias = conv_own(
        slots, there, count, core, tile_images, cotangent, conv_weights, layer_scale, expand_bias
    )
    keep, send = train(
        slots, there, count_there, core, acts, packed, conv_weights, layer_scale, expand_weight,
        bias, project_weight,
    )
    got = lax.ppermute(send, "slide", swap)
    pieces = arrange(place, keep, got)
    pieces = (
        [pieces[0]]
        + [along_x(pieces[step], step) for step in range(1, 4)]
        + [pieces[4]]
        + [along_y(pieces[4 + step], step) for step in range(1, 4)]
    )
    pieces = middle(place, *pieces)
    pieces = (
        [pieces[0]]
        + [along_y(pieces[step], step) for step in range(1, 4)]
        + [pieces[4]]
        + [along_x(pieces[4 + step], step) for step in range(1, 4)]
    )
    pieces = last(place, *pieces)
    total = pieces[0]
    for step in range(1, 8):
        total = total + along_z(pieces[step], step)
    return total[0], total[1]


def solution(mesh):
    in_specs = (
        P(("slide", "rep"), None, None, None),
        P(("slide", "rep"), None, None, None),
        P(),
        P(),
        P(),
        P(),
        P(),
        P(),
        P(),
        P(),
        P("slide", "rep"),
        P("slide", "rep", None),
    )
    out_specs = (P(("slide", "rep"), None), P(("slide", "rep"), None))
    return jax.shard_map(
        per_device, mesh=mesh, in_specs=in_specs, out_specs=out_specs, check_vma=False
    )
```

```python
import jax
import jax.numpy as jnp
from jax import lax
from jax.experimental import pallas as pl
from jax.experimental.pallas import tpu as pltpu
from jax.sharding import PartitionSpec as P

BANDS = 8
MARGIN = 3
BAND_ROWS = 4
BAND_TOK = 128
SLOTS = 16
GROUP = 2
KEPT = 9
ROWS = BAND_ROWS + 2 * MARGIN
HID_STEP = 768
SPAN = GROUP * BAND_TOK
GROUPS = SLOTS // GROUP
PAIRS = 8
CHUNK = 96
PART = 48
SHARE = 6

root_half = 0.7071067811865476
inv_root_tau = 0.3989422804014327

INNER = (((1,), (1,)), ((), ()))
PLAIN = (((1,), (0,)), ((), ()))


def half_copies(weight_hbm, weight, core, sems):
    copies = []
    for half in range(2):
        for pair in range(PAIRS):
            first = pl.multiple_of((2 * pair + (core ^ half)) * CHUNK, CHUNK)
            copies.append(
                pltpu.make_async_copy(
                    weight_hbm.at[pl.ds(first, CHUNK)],
                    weight.at[pl.ds((half * PAIRS + pair) * CHUNK, CHUNK)],
                    sems.at[half, pair],
                )
            )
    return copies


def pack_list(slots_ref, order_ref):
    listed = jnp.int32(0)
    for slot in range(SLOTS):
        block = slots_ref[slot]
        order_ref[listed] = jnp.maximum(block, 0)
        listed = listed + jnp.where(block >= 0, 1, 0)
    return listed


def block_copies(order_ref, index, images_hbm, cotan_hbm, images, cotans, sems):
    block = order_ref[index]
    tile = block // BANDS
    band = block % BANDS
    first = band * BAND_ROWS
    above = pltpu.make_async_copy(
        images_hbm.at[tile, pl.ds(first - MARGIN, MARGIN)], images.at[pl.ds(0, MARGIN)], sems.at[0]
    )
    middle = pltpu.make_async_copy(
        images_hbm.at[tile, pl.ds(first, BAND_ROWS)], images.at[pl.ds(MARGIN, BAND_ROWS)], sems.at[1]
    )
    below = pltpu.make_async_copy(
        images_hbm.at[tile, pl.ds(first + BAND_ROWS, MARGIN)],
        images.at[pl.ds(MARGIN + BAND_ROWS, MARGIN)],
        sems.at[2],
    )
    error = pltpu.make_async_copy(cotan_hbm.at[tile, pl.ds(first, BAND_ROWS)], cotans, sems.at[3])
    return band, above, middle, below, error


def start_block(band, above, middle, below, error):
    pl.when(band > 0)(above.start)
    middle.start()
    pl.when(band < BANDS - 1)(below.start)
    error.start()


def pack_kernel(slots_ref, images_hbm, cotan_hbm, packed, order_ref, sems):
    listed = pack_list(slots_ref, order_ref)

    def copies(index):
        place = packed.at[index - KEPT]
        return block_copies(
            order_ref,
            index,
            images_hbm,
            cotan_hbm,
            place.at[pl.ds(0, ROWS)],
            place.at[pl.ds(ROWS, BAND_ROWS)],
            sems.at[index],
        )

    @pl.loop(KEPT, listed)
    def _(index):
        start_block(*copies(index))

    @pl.loop(KEPT, listed)
    def _(index):
        band, above, middle, below, error = copies(index)
        pl.when(band > 0)(above.wait)
        middle.wait()
        pl.when(band < BANDS - 1)(below.wait)
        error.wait()


def conv_norm(image, band, taps, conv_out, depth_bias, gain, norm_bias):
    _, side, channels = image.shape

    @pl.when(band == 0)
    def _():
        image[:MARGIN] = jnp.zeros((MARGIN, side, channels), image.dtype)

    @pl.when(band == BANDS - 1)
    def _():
        image[MARGIN + BAND_ROWS : ROWS] = jnp.zeros((MARGIN, side, channels), image.dtype)

    column = lax.broadcasted_iota(jnp.int32, (side, 128), 0)
    for lanes in range(0, channels, 128):
        part = slice(lanes, lanes + 128)
        for row in range(BAND_ROWS):
            sums = [None] * 7
            for dy in range(7):
                x = image[row + dy, :, part].astype(jnp.float32)
                for dx in range(7):
                    term = x * taps[dy, dx : dx + 1, part]
                    sums[dx] = term if sums[dx] is None else sums[dx] + term
            total = sums[MARGIN] + depth_bias[:, part]
            for dx in range(-MARGIN, MARGIN + 1):
                if dx != 0:
                    moved = pltpu.roll(sums[dx + MARGIN], (-dx) % side, 0)
                    inside = (column + dx >= 0) & (column + dx < side)
                    total = total + jnp.where(inside, moved, 0.0)
            conv_out[row * side : (row + 1) * side, part] = total
    mixed = conv_out[...]
    centre = jnp.mean(mixed, axis=-1, keepdims=True)
    away = mixed - centre
    spread = jnp.mean(away * away, axis=-1, keepdims=True)
    return (away * lax.rsqrt(spread + 1e-06) * gain + norm_bias).astype(jnp.bfloat16)


def scale_errors(errors, scale):
    rows, side, channels = errors.shape
    flat = errors[...].reshape(rows * side, channels)
    return (flat.astype(jnp.float32) * scale).astype(jnp.bfloat16)


def conv_kernel(
    slots_ref,
    count_ref,
    core_ref,
    images_hbm,
    cotan_hbm,
    taps_ref,
    depth_bias_ref,
    gain_ref,
    norm_bias_ref,
    scale_ref,
    expand_bias_ref,
    acts_hbm,
    bias_ref,
    images,
    cotans,
    taps,
    acts,
    conv_out,
    bias_all,
    order_ref,
    image_sems,
    acts_sems,
):
    channels = images_hbm.shape[3]
    core = core_ref[0]
    own = jnp.minimum(pack_list(slots_ref, order_ref), KEPT)

    def copies(index):
        return block_copies(
            order_ref,
            index,
            images_hbm,
            cotan_hbm,
            images.at[index],
            cotans.at[index],
            image_sems.at[index],
        )

    @pl.loop(0, own)
    def _(index):
        start_block(*copies(index))

    taps[...] = taps_ref[...].astype(jnp.float32)
    hidden = expand_bias_ref.shape[0]
    for first in range(0, hidden, 128):
        row = expand_bias_ref[pl.ds(first, 128)].reshape(1, 128)
        bias_all[pl.ds(first, 128), :] = jnp.broadcast_to(row, (128, 128)).T
    for half in range(2):
        for pair in range(PAIRS):
            rows = pl.ds(pl.multiple_of((2 * pair + (core ^ half)) * CHUNK, CHUNK), CHUNK)
            bias_ref[pl.ds((half * PAIRS + pair) * CHUNK, CHUNK), :] = bias_all[rows, :]

    depth_bias = depth_bias_ref[...].reshape(1, channels)
    gain = gain_ref[...].reshape(1, channels)
    norm_bias = norm_bias_ref[...].reshape(1, channels)
    scale = scale_ref[...].reshape(1, channels) / count_ref[0].astype(jnp.float32)

    def acts_copy(index):
        rows = pl.ds(pl.multiple_of(index * BAND_TOK, BAND_TOK), BAND_TOK)
        return pltpu.make_async_copy(acts.at[:, rows], acts_hbm.at[:, rows], acts_sems.at[index])

    @pl.loop(0, own)
    def _(index):
        band, above, middle, below, error = copies(index)
        pl.when(band > 0)(above.wait)
        middle.wait()
        pl.when(band < BANDS - 1)(below.wait)
        rows = pl.ds(pl.multiple_of(index * BAND_TOK, BAND_TOK), BAND_TOK)
        acts[0, rows, :] = conv_norm(
            images.at[index], band, taps, conv_out, depth_bias, gain, norm_bias
        )
        error.wait()
        acts[1, rows, :] = scale_errors(cotans.at[index], scale)
        acts_copy(index).start()

    @pl.loop(0, own)
    def _(index):
        acts_copy(index).wait()


def train_kernel(
    slots_ref,
    there_ref,
    count_there_ref,
    core_ref,
    acts_hbm,
    packed_hbm,
    taps_ref,
    depth_bias_ref,
    gain_ref,
    norm_bias_ref,
    scale_ref,
    expand_hbm,
    bias_ref,
    project_hbm,
    keep_ref,
    send_ref,
    packed,
    taps,
    acts,
    conv_out,
    expand,
    project,
    grad,
    order_ref,
    packed_sems,
    acts_sems,
    weight_sems,
):
    channels = packed_hbm.shape[3]
    core = core_ref[0]
    listed_there = pack_list(there_ref, order_ref)
    listed = jnp.int32(0)
    for slot in range(SLOTS):
        listed = listed + jnp.where(slots_ref[slot] >= 0, 1, 0)
    own = jnp.minimum(listed, KEPT)
    taken = jnp.maximum(listed_there - KEPT, 0)

    def packed_copy(place):
        return pltpu.make_async_copy(packed_hbm.at[place], packed.at[place], packed_sems.at[place])

    def acts_copy(index):
        rows = pl.ds(pl.multiple_of(index * BAND_TOK, BAND_TOK), BAND_TOK)
        return pltpu.make_async_copy(acts_hbm.at[:, rows], acts.at[:, rows], acts_sems.at[index])

    @pl.loop(0, taken)
    def _(index):
        packed_copy(index).start()

    weight_copies = half_copies(expand_hbm, expand, core, weight_sems.at[0])
    weight_copies += half_copies(project_hbm, project, core, weight_sems.at[1])
    for copy in weight_copies:
        copy.start()

    @pl.loop(0, own)
    def _(index):
        acts_copy(index).start()

    taps[...] = taps_ref[...].astype(jnp.float32)
    depth_bias = depth_bias_ref[...].reshape(1, channels)
    gain = gain_ref[...].reshape(1, channels)
    norm_bias = norm_bias_ref[...].reshape(1, channels)
    scale = scale_ref[...].reshape(1, channels) / count_there_ref[0].astype(jnp.float32)
    keep_ref[...] = jnp.zeros(keep_ref.shape, jnp.float32)
    grad[...] = jnp.zeros(grad.shape, jnp.float32)

    @pl.loop(0, taken)
    def _(index):
        packed_copy(index).wait()
        rows = pl.ds(pl.multiple_of((own + index) * BAND_TOK, BAND_TOK), BAND_TOK)
        band = order_ref[KEPT + index] % BANDS
        acts[0, rows, :] = conv_norm(
            packed.at[index, pl.ds(0, ROWS)], band, taps, conv_out, depth_bias, gain, norm_bias
        )
        acts[1, rows, :] = scale_errors(packed.at[index, pl.ds(ROWS, BAND_ROWS)], scale)

    total = own + taken

    @pl.when(total % GROUP != 0)
    def _():
        rows = pl.ds(pl.multiple_of(total * BAND_TOK, BAND_TOK), BAND_TOK)
        acts[:, rows, :] = jnp.zeros((2, BAND_TOK, channels), acts.dtype)

    for copy in weight_copies:
        copy.wait()

    @pl.loop(0, own)
    def _(index):
        acts_copy(index).wait()

    half = keep_ref.shape[1]

    @pl.loop(0, (total + GROUP - 1) // GROUP)
    def _(group):
        rows = pl.ds(pl.multiple_of(group * SPAN, SPAN), SPAN)
        flat_in = acts[0, rows, :]
        flat_err = acts[1, rows, :]
        for start in range(0, 2 * half, HID_STEP):
            units = slice(start, start + HID_STEP)
            pre_act = lax.dot_general(
                expand[units, :], flat_in, INNER, preferred_element_type=jnp.float32
            )
            back_grad = lax.dot_general(
                project[units, :], flat_err, INNER, preferred_element_type=jnp.float32
            )
            pre_act = pre_act + jnp.concatenate([bias_ref[units, :]] * (SPAN // 128), axis=1)
            share = 0.5 * (1.0 + lax.erf(pre_act * root_half))
            activated = (pre_act * share).astype(jnp.bfloat16)
            bell = jnp.exp(-0.5 * pre_act * pre_act) * inv_root_tau
            slope_term = (back_grad * (share + pre_act * bell)).astype(jnp.bfloat16)
            sums, first = (keep_ref, start) if start < half else (grad, start - half)
            units = slice(first, first + HID_STEP)
            sums[0, units, :] += lax.dot_general(
                slope_term, flat_in, PLAIN, preferred_element_type=jnp.float32
            )
            sums[1, units, :] += lax.dot_general(
                activated, flat_err, PLAIN, preferred_element_type=jnp.float32
            )

    send_ref[...] = grad[...].astype(send_ref.dtype)


SMEM = pl.BlockSpec(memory_space=pltpu.SMEM)
VMEM = pl.BlockSpec(memory_space=pltpu.VMEM)
HBM = pl.BlockSpec(memory_space=pl.ANY)


def params(mib):
    return pltpu.CompilerParams(vmem_limit_bytes=mib * 2**20)


def pack(slots, tile_images, cotangent):
    side, channels = tile_images.shape[1], tile_images.shape[3]
    return pl.pallas_call(
        pack_kernel,
        out_shape=jax.ShapeDtypeStruct(
            (SLOTS - KEPT, ROWS + BAND_ROWS, side, channels), jnp.bfloat16
        ),
        in_specs=[SMEM, HBM, HBM],
        out_specs=VMEM,
        scratch_shapes=[
            pltpu.SMEM((SLOTS + 1,), jnp.int32),
            pltpu.SemaphoreType.DMA((SLOTS, 4)),
        ],
        compiler_params=params(56),
        name="pack",
    )(slots, tile_images, cotangent)


def conv_own(slots, count, core, tile_images, cotangent, conv_weights, scale, expand_bias):
    side, channels = tile_images.shape[1], tile_images.shape[3]
    hidden = expand_bias.shape[0]
    bf16, f32 = jnp.bfloat16, jnp.float32
    return pl.pallas_call(
        conv_kernel,
        out_shape=(
            jax.ShapeDtypeStruct((2, KEPT * BAND_TOK, channels), bf16),
            jax.ShapeDtypeStruct((hidden, 128), f32),
        ),
        in_specs=[SMEM] * 3 + [HBM] * 2 + [VMEM] * 6,
        out_specs=[HBM, VMEM],
        scratch_shapes=[
            pltpu.VMEM((KEPT, ROWS, side, channels), bf16),
            pltpu.VMEM((KEPT, BAND_ROWS, side, channels), bf16),
            pltpu.VMEM((7, 7, channels), f32),
            pltpu.VMEM((2, KEPT * BAND_TOK, channels), bf16),
            pltpu.VMEM((BAND_TOK, channels), f32),
            pltpu.VMEM((hidden, 128), f32),
            pltpu.SMEM((SLOTS + 1,), jnp.int32),
            pltpu.SemaphoreType.DMA((SLOTS, 4)),
            pltpu.SemaphoreType.DMA((SLOTS,)),
        ],
        compiler_params=params(56),
        cost_estimate=pl.CostEstimate(flops=8 * 10**9, bytes_accessed=10**7, transcendentals=0),
        name="conv_own",
    )(slots, count, core, tile_images, cotangent, *conv_weights, scale, expand_bias)


def train(
    slots, there, count_there, core, acts, packed, conv_weights, scale, expand_weight, bias,
    project_weight,
):
    hidden, channels = expand_weight.shape
    half = hidden // 2
    bf16, f32 = jnp.bfloat16, jnp.float32
    return pl.pallas_call(
        train_kernel,
        out_shape=(
            jax.ShapeDtypeStruct((2, half, channels), f32),
            jax.ShapeDtypeStruct((2, half, channels), bf16),
        ),
        in_specs=[SMEM] * 4 + [HBM] * 2 + [VMEM] * 5 + [HBM, VMEM, HBM],
        out_specs=[VMEM, VMEM],
        scratch_shapes=[
            pltpu.VMEM(packed.shape, bf16),
            pltpu.VMEM((7, 7, channels), f32),
            pltpu.VMEM((2, SLOTS * BAND_TOK, channels), bf16),
            pltpu.VMEM((BAND_TOK, channels), f32),
            pltpu.VMEM((hidden, channels), bf16),
            pltpu.VMEM((hidden, channels), bf16),
            pltpu.VMEM((2, half, channels), f32),
            pltpu.SMEM((SLOTS + 1,), jnp.int32),
            pltpu.SemaphoreType.DMA((SLOTS - KEPT,)),
            pltpu.SemaphoreType.DMA((SLOTS,)),
            pltpu.SemaphoreType.DMA((2, 2, PAIRS)),
        ],
        compiler_params=params(56),
        cost_estimate=pl.CostEstimate(flops=9 * 10**9, bytes_accessed=10**7, transcendentals=0),
        name="train",
    )(
        slots, there, count_there, core, acts, packed, *conv_weights, scale, expand_weight, bias,
        project_weight,
    )


def arrange_kernel(place_ref, keep_ref, got_ref, *refs):
    in_keep, in_send, out_keep, out_send = refs[0], refs[1:4], refs[4], refs[5:8]
    sums = refs[8]
    new = lax.broadcasted_iota(jnp.int32, (CHUNK, CHUNK), 0)
    old = lax.broadcasted_iota(jnp.int32, (CHUNK, CHUNK), 1)
    share = (new * 43) >> 8
    source = ((share & 7) * 2 + (share >> 3)) * SHARE + (new - share * SHARE)
    move = jnp.where(old == source, 1.0, 0.0).astype(jnp.bfloat16)
    for which in range(2):
        for pair in range(PAIRS):
            rows = slice(pair * CHUNK, (pair + 1) * CHUNK)
            total = keep_ref[which, rows, :] + got_ref[which, rows, :].astype(jnp.float32)
            high = total.astype(jnp.bfloat16)
            low = (total - high.astype(jnp.float32)).astype(jnp.bfloat16)
            moved = lax.dot_general(
                move, high, PLAIN, preferred_element_type=jnp.float32
            ) + lax.dot_general(move, low, PLAIN, preferred_element_type=jnp.float32)
            x, y_high = pair // 2, pair % 2
            for y_low in range(2):
                piece = moved[y_low * PART : (y_low + 1) * PART]
                if which == 0:
                    sums[0, x, 2 * y_high + y_low] = piece
                else:
                    sums[1, 2 * y_high + y_low, x] = piece
    for which, keep, send in ((0, in_keep, in_send), (1, out_keep, out_send)):
        here = place_ref[which]
        keep[...] = sums[which, here]
        for step in range(1, 4):
            there = (here + step) & 3
            send[step - 1][...] = sums[which, there].astype(jnp.bfloat16)


def arrange(place, keep, got):
    channels = keep.shape[-1]
    own = jax.ShapeDtypeStruct((4, PART, channels), jnp.float32)
    away = jax.ShapeDtypeStruct((4, PART, channels), jnp.bfloat16)
    return pl.pallas_call(
        arrange_kernel,
        out_shape=[own, away, away, away, own, away, away, away],
        in_specs=[SMEM, VMEM, VMEM],
        out_specs=[VMEM] * 8,
        scratch_shapes=[pltpu.VMEM((2, 4, 4, PART, channels), jnp.float32)],
        compiler_params=params(14),
        name="arrange",
    )(place, keep, got)


def middle_kernel(place_ref, *refs):
    ins, outs, sums = refs[:8], refs[8:16], refs[16]
    for which in range(2):
        keep, got = ins[4 * which], ins[4 * which + 1 : 4 * which + 4]
        total = keep[...]
        for piece in got:
            total = total + piece[...].astype(jnp.float32)
        sums[which] = total
        here = place_ref[1 - which]
        outs[4 * which][...] = sums[which, here]
        for step in range(1, 4):
            there = (here + step) & 3
            outs[4 * which + step][...] = sums[which, there].astype(jnp.bfloat16)


def middle(place, *ins):
    channels = ins[0].shape[-1]
    own = jax.ShapeDtypeStruct((PART, channels), jnp.float32)
    away = jax.ShapeDtypeStruct((PART, channels), jnp.bfloat16)
    return pl.pallas_call(
        middle_kernel,
        out_shape=[own, away, away, away] * 2,
        in_specs=[SMEM] + [VMEM] * 8,
        out_specs=[VMEM] * 8,
        scratch_shapes=[pltpu.VMEM((2, 4, PART, channels), jnp.float32)],
        compiler_params=params(6),
        name="middle",
    )(place, *ins)


def last_kernel(place_ref, *refs):
    ins, outs, sums = refs[:8], refs[8:16], refs[16]
    for which in range(2):
        total = ins[4 * which][...]
        for piece in ins[4 * which + 1 : 4 * which + 4]:
            total = total + piece[...].astype(jnp.float32)
        for z in range(8):
            sums[z, which] = total[z * SHARE : (z + 1) * SHARE]
    here = place_ref[2]
    for step in range(8):
        outs[step][...] = sums[(here + step) & 7]


def last(place, *ins):
    channels = ins[0].shape[-1]
    piece = jax.ShapeDtypeStruct((2, SHARE, channels), jnp.float32)
    return pl.pallas_call(
        last_kernel,
        out_shape=[piece] * 8,
        in_specs=[SMEM] + [VMEM] * 8,
        out_specs=[VMEM] * 8,
        scratch_shapes=[pltpu.VMEM((8, 2, SHARE, channels), jnp.float32)],
        compiler_params=params(4),
        name="last",
    )(place, *ins)


def along_x(a, step):
    return lax.ppermute(a, "slide", [(i, (i + 4 * step) % 16) for i in range(16)])


def along_y(a, step):
    pairs = []
    for s in range(16):
        for r in range(16):
            to = ((s // 2) % 2 * 2 + r % 2 + step) % 4
            pairs.append((s * 16 + r, ((s & ~2) | (to // 2 * 2)) * 16 + ((r & ~1) | to % 2)))
    return lax.ppermute(a, ("slide", "rep"), pairs)


def along_z(a, step):
    return lax.ppermute(a, "rep", [(i, (i + 2 * step) % 16) for i in range(16)])


def per_device(
    tile_images,
    cotangent,
    depth_kernel,
    depth_bias,
    norm_gain,
    norm_bias,
    expand_weight,
    expand_bias,
    project_weight,
    layer_scale,
    tile_counts,
    send_list,
):
    slide, rep = lax.axis_index("slide"), lax.axis_index("rep")
    place = jnp.stack([slide // 4, (slide // 2) % 2 * 2 + rep % 2, rep // 2]).astype(jnp.int32)
    core = lax.rem(slide, 2).astype(jnp.int32).reshape(1)
    slots = send_list.reshape(-1)
    count = tile_counts.reshape(-1)
    conv_weights = (depth_kernel, depth_bias, norm_gain, norm_bias)
    swap = [(i, i ^ 1) for i in range(16)]
    there = lax.ppermute(slots, "slide", swap)
    count_there = lax.ppermute(count, "slide", swap)
    packed = lax.ppermute(pack(slots, tile_images, cotangent), "slide", swap)
    acts, bias = conv_own(
        slots, count, core, tile_images, cotangent, conv_weights, layer_scale, expand_bias
    )
    keep, send = train(
        slots, there, count_there, core, acts, packed, conv_weights, layer_scale, expand_weight,
        bias, project_weight,
    )
    got = lax.ppermute(send, "slide", swap)
    pieces = arrange(place, keep, got)
    pieces = (
        [pieces[0]]
        + [along_x(pieces[step], step) for step in range(1, 4)]
        + [pieces[4]]
        + [along_y(pieces[4 + step], step) for step in range(1, 4)]
    )
    pieces = middle(place, *pieces)
    pieces = (
        [pieces[0]]
        + [along_y(pieces[step], step) for step in range(1, 4)]
        + [pieces[4]]
        + [along_x(pieces[4 + step], step) for step in range(1, 4)]
    )
    pieces = last(place, *pieces)
    total = pieces[0]
    for step in range(1, 8):
        total = total + along_z(pieces[step], step)
    return total[0], total[1]


def solution(mesh):
    in_specs = (
        P(("slide", "rep"), None, None, None),
        P(("slide", "rep"), None, None, None),
        P(),
        P(),
        P(),
        P(),
        P(),
        P(),
        P(),
        P(),
        P("slide", "rep"),
        P("slide", "rep", None),
    )
    out_specs = (P(("slide", "rep"), None), P(("slide", "rep"), None))
    return jax.shard_map(
        per_device, mesh=mesh, in_specs=in_specs, out_specs=out_specs, check_vma=False
    )
```

```python
import jax
import jax.numpy as jnp
from jax import lax
from jax.experimental import pallas as pl
from jax.experimental.pallas import tpu as pltpu
from jax.sharding import PartitionSpec as P

BANDS = 8
MARGIN = 3
BAND_ROWS = 4
BAND_TOK = 128
SLOTS = 16
GROUP = 2
KEPT = 9
ROWS = BAND_ROWS + 2 * MARGIN
HID_STEP = 768
SPAN = GROUP * BAND_TOK
GROUPS = SLOTS // GROUP
PAIRS = 8
CHUNK = 96
SLAB = 2 * CHUNK
PLANE = 32
SHARE = 6
DEAL = 16

root_half = 0.7071067811865476
inv_root_tau = 0.3989422804014327

INNER = (((1,), (1,)), ((), ()))
PLAIN = (((1,), (0,)), ((), ()))


def half_copies(weight_hbm, weight, core, sems):
    copies = []
    for half in range(2):
        for pair in range(PAIRS):
            first = pl.multiple_of((2 * pair + (core ^ half)) * CHUNK, CHUNK)
            copies.append(
                pltpu.make_async_copy(
                    weight_hbm.at[pl.ds(first, CHUNK)],
                    weight.at[pl.ds((half * PAIRS + pair) * CHUNK, CHUNK)],
                    sems.at[half, pair],
                )
            )
    return copies


def pack_list(slots_ref, order_ref):
    listed = jnp.int32(0)
    for slot in range(SLOTS):
        block = slots_ref[slot]
        order_ref[listed] = jnp.maximum(block, 0)
        listed = listed + jnp.where(block >= 0, 1, 0)
    return listed


def block_copies(order_ref, index, images_hbm, cotan_hbm, images, cotans, sems):
    block = order_ref[index]
    tile = block // BANDS
    band = block % BANDS
    first = band * BAND_ROWS
    above = pltpu.make_async_copy(
        images_hbm.at[tile, pl.ds(first - MARGIN, MARGIN)], images.at[pl.ds(0, MARGIN)], sems.at[0]
    )
    middle = pltpu.make_async_copy(
        images_hbm.at[tile, pl.ds(first, BAND_ROWS)], images.at[pl.ds(MARGIN, BAND_ROWS)], sems.at[1]
    )
    below = pltpu.make_async_copy(
        images_hbm.at[tile, pl.ds(first + BAND_ROWS, MARGIN)],
        images.at[pl.ds(MARGIN + BAND_ROWS, MARGIN)],
        sems.at[2],
    )
    error = pltpu.make_async_copy(cotan_hbm.at[tile, pl.ds(first, BAND_ROWS)], cotans, sems.at[3])
    return band, above, middle, below, error


def start_block(band, above, middle, below, error):
    pl.when(band > 0)(above.start)
    middle.start()
    pl.when(band < BANDS - 1)(below.start)
    error.start()


def pack_kernel(slots_ref, images_hbm, cotan_hbm, packed_hbm, packed, order_ref, sems, out_sems):
    listed = pack_list(slots_ref, order_ref)

    def copies(index):
        place = packed.at[index - KEPT]
        return block_copies(
            order_ref,
            index,
            images_hbm,
            cotan_hbm,
            place.at[pl.ds(0, ROWS)],
            place.at[pl.ds(ROWS, BAND_ROWS)],
            sems.at[index],
        )

    def out_copy(index):
        place = index - KEPT
        return pltpu.make_async_copy(packed.at[place], packed_hbm.at[place], out_sems.at[place])

    @pl.loop(KEPT, listed)
    def _(index):
        start_block(*copies(index))

    @pl.loop(KEPT, listed)
    def _(index):
        band, above, middle, below, error = copies(index)
        pl.when(band > 0)(above.wait)
        middle.wait()
        pl.when(band < BANDS - 1)(below.wait)
        error.wait()
        out_copy(index).start()

    @pl.loop(KEPT, listed)
    def _(index):
        out_copy(index).wait()


def conv_norm(image, band, taps, conv_out, depth_bias, gain, norm_bias):
    _, side, channels = image.shape

    @pl.when(band == 0)
    def _():
        image[:MARGIN] = jnp.zeros((MARGIN, side, channels), image.dtype)

    @pl.when(band == BANDS - 1)
    def _():
        image[MARGIN + BAND_ROWS : ROWS] = jnp.zeros((MARGIN, side, channels), image.dtype)

    column = lax.broadcasted_iota(jnp.int32, (side, 128), 0)
    for lanes in range(0, channels, 128):
        part = slice(lanes, lanes + 128)
        for row in range(BAND_ROWS):
            sums = [None] * 7
            for dy in range(7):
                x = image[row + dy, :, part].astype(jnp.float32)
                for dx in range(7):
                    term = x * taps[dy, dx : dx + 1, part]
                    sums[dx] = term if sums[dx] is None else sums[dx] + term
            total = sums[MARGIN] + depth_bias[:, part]
            for dx in range(-MARGIN, MARGIN + 1):
                if dx != 0:
                    moved = pltpu.roll(sums[dx + MARGIN], (-dx) % side, 0)
                    inside = (column + dx >= 0) & (column + dx < side)
                    total = total + jnp.where(inside, moved, 0.0)
            conv_out[row * side : (row + 1) * side, part] = total
    mixed = conv_out[...]
    centre = jnp.mean(mixed, axis=-1, keepdims=True)
    away = mixed - centre
    spread = jnp.mean(away * away, axis=-1, keepdims=True)
    return (away * lax.rsqrt(spread + 1e-06) * gain + norm_bias).astype(jnp.bfloat16)


def scale_errors(errors, scale):
    rows, side, channels = errors.shape
    flat = errors[...].reshape(rows * side, channels)
    return (flat.astype(jnp.float32) * scale).astype(jnp.bfloat16)


def conv_kernel(
    slots_ref,
    count_ref,
    core_ref,
    images_hbm,
    cotan_hbm,
    taps_ref,
    depth_bias_ref,
    gain_ref,
    norm_bias_ref,
    scale_ref,
    expand_bias_ref,
    acts_hbm,
    bias_ref,
    images,
    cotans,
    taps,
    acts,
    conv_out,
    bias_all,
    order_ref,
    image_sems,
    acts_sems,
):
    channels = images_hbm.shape[3]
    core = core_ref[0]
    own = jnp.minimum(pack_list(slots_ref, order_ref), KEPT)

    def copies(index):
        return block_copies(
            order_ref,
            index,
            images_hbm,
            cotan_hbm,
            images.at[index],
            cotans.at[index],
            image_sems.at[index],
        )

    @pl.loop(0, own)
    def _(index):
        start_block(*copies(index))

    taps[...] = taps_ref[...].astype(jnp.float32)
    hidden = expand_bias_ref.shape[0]
    for first in range(0, hidden, 128):
        row = expand_bias_ref[pl.ds(first, 128)].reshape(1, 128)
        bias_all[pl.ds(first, 128), :] = jnp.broadcast_to(row, (128, 128)).T
    for half in range(2):
        for pair in range(PAIRS):
            rows = pl.ds(pl.multiple_of((2 * pair + (core ^ half)) * CHUNK, CHUNK), CHUNK)
            bias_ref[pl.ds((half * PAIRS + pair) * CHUNK, CHUNK), :] = bias_all[rows, :]

    depth_bias = depth_bias_ref[...].reshape(1, channels)
    gain = gain_ref[...].reshape(1, channels)
    norm_bias = norm_bias_ref[...].reshape(1, channels)
    scale = scale_ref[...].reshape(1, channels) / count_ref[0].astype(jnp.float32)

    def acts_copy(index):
        rows = pl.ds(pl.multiple_of(index * BAND_TOK, BAND_TOK), BAND_TOK)
        return pltpu.make_async_copy(acts.at[:, rows], acts_hbm.at[:, rows], acts_sems.at[index])

    @pl.loop(0, own)
    def _(index):
        band, above, middle, below, error = copies(index)
        pl.when(band > 0)(above.wait)
        middle.wait()
        pl.when(band < BANDS - 1)(below.wait)
        rows = pl.ds(pl.multiple_of(index * BAND_TOK, BAND_TOK), BAND_TOK)
        acts[0, rows, :] = conv_norm(
            images.at[index], band, taps, conv_out, depth_bias, gain, norm_bias
        )
        error.wait()
        acts[1, rows, :] = scale_errors(cotans.at[index], scale)
        acts_copy(index).start()

    @pl.loop(0, own)
    def _(index):
        acts_copy(index).wait()


def train_kernel(
    slots_ref,
    there_ref,
    count_there_ref,
    core_ref,
    acts_hbm,
    packed_hbm,
    taps_ref,
    depth_bias_ref,
    gain_ref,
    norm_bias_ref,
    scale_ref,
    expand_hbm,
    bias_ref,
    project_hbm,
    keep_ref,
    send_ref,
    packed,
    taps,
    acts,
    conv_out,
    expand,
    project,
    grad,
    order_ref,
    packed_sems,
    acts_sems,
    weight_sems,
):
    channels = packed_hbm.shape[3]
    core = core_ref[0]
    listed_there = pack_list(there_ref, order_ref)
    listed = jnp.int32(0)
    for slot in range(SLOTS):
        listed = listed + jnp.where(slots_ref[slot] >= 0, 1, 0)
    own = jnp.minimum(listed, KEPT)
    taken = jnp.maximum(listed_there - KEPT, 0)

    def packed_copy(place):
        return pltpu.make_async_copy(packed_hbm.at[place], packed.at[place], packed_sems.at[place])

    def acts_copy(index):
        rows = pl.ds(pl.multiple_of(index * BAND_TOK, BAND_TOK), BAND_TOK)
        return pltpu.make_async_copy(acts_hbm.at[:, rows], acts.at[:, rows], acts_sems.at[index])

    @pl.loop(0, taken)
    def _(index):
        packed_copy(index).start()

    weight_copies = half_copies(expand_hbm, expand, core, weight_sems.at[0])
    weight_copies += half_copies(project_hbm, project, core, weight_sems.at[1])
    for copy in weight_copies:
        copy.start()

    @pl.loop(0, own)
    def _(index):
        acts_copy(index).start()

    taps[...] = taps_ref[...].astype(jnp.float32)
    depth_bias = depth_bias_ref[...].reshape(1, channels)
    gain = gain_ref[...].reshape(1, channels)
    norm_bias = norm_bias_ref[...].reshape(1, channels)
    scale = scale_ref[...].reshape(1, channels) / count_there_ref[0].astype(jnp.float32)
    grad[...] = jnp.zeros(grad.shape, jnp.float32)

    @pl.loop(0, taken)
    def _(index):
        packed_copy(index).wait()
        rows = pl.ds(pl.multiple_of((own + index) * BAND_TOK, BAND_TOK), BAND_TOK)
        band = order_ref[KEPT + index] % BANDS
        acts[0, rows, :] = conv_norm(
            packed.at[index, pl.ds(0, ROWS)], band, taps, conv_out, depth_bias, gain, norm_bias
        )
        acts[1, rows, :] = scale_errors(packed.at[index, pl.ds(ROWS, BAND_ROWS)], scale)

    total = own + taken

    @pl.when(total % GROUP != 0)
    def _():
        rows = pl.ds(pl.multiple_of(total * BAND_TOK, BAND_TOK), BAND_TOK)
        acts[:, rows, :] = jnp.zeros((2, BAND_TOK, channels), acts.dtype)

    for copy in weight_copies:
        copy.wait()

    @pl.loop(0, own)
    def _(index):
        acts_copy(index).wait()

    half = keep_ref.shape[1]

    @pl.loop(0, (total + GROUP - 1) // GROUP)
    def _(group):
        rows = pl.ds(pl.multiple_of(group * SPAN, SPAN), SPAN)
        flat_in = acts[0, rows, :]
        flat_err = acts[1, rows, :]
        for start in range(0, 2 * half, HID_STEP):
            units = slice(start, start + HID_STEP)
            pre_act = lax.dot_general(
                expand[units, :], flat_in, INNER, preferred_element_type=jnp.float32
            )
            back_grad = lax.dot_general(
                project[units, :], flat_err, INNER, preferred_element_type=jnp.float32
            )
            pre_act = pre_act + jnp.concatenate([bias_ref[units, :]] * (SPAN // 128), axis=1)
            share = 0.5 * (1.0 + lax.erf(pre_act * root_half))
            activated = (pre_act * share).astype(jnp.bfloat16)
            bell = jnp.exp(-0.5 * pre_act * pre_act) * inv_root_tau
            slope_term = (back_grad * (share + pre_act * bell)).astype(jnp.bfloat16)
            grad[0, units, :] += lax.dot_general(
                slope_term, flat_in, PLAIN, preferred_element_type=jnp.float32
            )
            grad[1, units, :] += lax.dot_general(
                activated, flat_err, PLAIN, preferred_element_type=jnp.float32
            )

    keep_ref[...] = grad[:, :half, :].astype(keep_ref.dtype)
    send_ref[...] = grad[:, half:, :].astype(send_ref.dtype)


SMEM = pl.BlockSpec(memory_space=pltpu.SMEM)
VMEM = pl.BlockSpec(memory_space=pltpu.VMEM)
HBM = pl.BlockSpec(memory_space=pl.ANY)


def params(mib):
    return pltpu.CompilerParams(vmem_limit_bytes=mib * 2**20)


def pack(slots, tile_images, cotangent):
    side, channels = tile_images.shape[1], tile_images.shape[3]
    return pl.pallas_call(
        pack_kernel,
        out_shape=jax.ShapeDtypeStruct(
            (SLOTS - KEPT, ROWS + BAND_ROWS, side, channels), jnp.bfloat16
        ),
        in_specs=[SMEM, HBM, HBM],
        out_specs=HBM,
        scratch_shapes=[
            pltpu.VMEM((SLOTS - KEPT, ROWS + BAND_ROWS, side, channels), jnp.bfloat16),
            pltpu.SMEM((SLOTS + 1,), jnp.int32),
            pltpu.SemaphoreType.DMA((SLOTS, 4)),
            pltpu.SemaphoreType.DMA((SLOTS - KEPT,)),
        ],
        compiler_params=params(56),
        name="pack",
    )(slots, tile_images, cotangent)


def conv_own(slots, count, core, tile_images, cotangent, conv_weights, scale, expand_bias):
    side, channels = tile_images.shape[1], tile_images.shape[3]
    hidden = expand_bias.shape[0]
    bf16, f32 = jnp.bfloat16, jnp.float32
    return pl.pallas_call(
        conv_kernel,
        out_shape=(
            jax.ShapeDtypeStruct((2, KEPT * BAND_TOK, channels), bf16),
            jax.ShapeDtypeStruct((hidden, 128), f32),
        ),
        in_specs=[SMEM] * 3 + [HBM] * 2 + [VMEM] * 6,
        out_specs=[HBM, VMEM],
        scratch_shapes=[
            pltpu.VMEM((KEPT, ROWS, side, channels), bf16),
            pltpu.VMEM((KEPT, BAND_ROWS, side, channels), bf16),
            pltpu.VMEM((7, 7, channels), f32),
            pltpu.VMEM((2, KEPT * BAND_TOK, channels), bf16),
            pltpu.VMEM((BAND_TOK, channels), f32),
            pltpu.VMEM((hidden, 128), f32),
            pltpu.SMEM((SLOTS + 1,), jnp.int32),
            pltpu.SemaphoreType.DMA((SLOTS, 4)),
            pltpu.SemaphoreType.DMA((SLOTS,)),
        ],
        compiler_params=params(56),
        cost_estimate=pl.CostEstimate(flops=8 * 10**9, bytes_accessed=10**7, transcendentals=0),
        name="conv_own",
    )(slots, count, core, tile_images, cotangent, *conv_weights, scale, expand_bias)


def train(
    slots, there, count_there, core, acts, packed, conv_weights, scale, expand_weight, bias,
    project_weight,
):
    hidden, channels = expand_weight.shape
    half = hidden // 2
    bf16, f32 = jnp.bfloat16, jnp.float32
    return pl.pallas_call(
        train_kernel,
        out_shape=(
            jax.ShapeDtypeStruct((2, half, channels), bf16),
            jax.ShapeDtypeStruct((2, half, channels), bf16),
        ),
        in_specs=[SMEM] * 4 + [HBM] * 2 + [VMEM] * 5 + [HBM, VMEM, HBM],
        out_specs=[VMEM, VMEM],
        scratch_shapes=[
            pltpu.VMEM(packed.shape, bf16),
            pltpu.VMEM((7, 7, channels), f32),
            pltpu.VMEM((2, SLOTS * BAND_TOK, channels), bf16),
            pltpu.VMEM((BAND_TOK, channels), f32),
            pltpu.VMEM((hidden, channels), bf16),
            pltpu.VMEM((hidden, channels), bf16),
            pltpu.VMEM((2, hidden, channels), f32),
            pltpu.SMEM((SLOTS + 1,), jnp.int32),
            pltpu.SemaphoreType.DMA((SLOTS - KEPT,)),
            pltpu.SemaphoreType.DMA((SLOTS,)),
            pltpu.SemaphoreType.DMA((2, 2, PAIRS)),
        ],
        compiler_params=params(56),
        cost_estimate=pl.CostEstimate(flops=9 * 10**9, bytes_accessed=10**7, transcendentals=0),
        name="train",
    )(
        slots, there, count_there, core, acts, packed, *conv_weights, scale, expand_weight, bias,
        project_weight,
    )


def split_kernel(place_ref, keep_ref, got_ref, own_ref, *send):
    here = place_ref[0]
    for step in range(4):
        rows = pl.ds(pl.multiple_of(((here + step) & 3) * SLAB, SLAB), SLAB)
        total = keep_ref[:, rows, :].astype(jnp.float32) + got_ref[:, rows, :].astype(jnp.float32)
        if step == 0:
            own_ref[...] = total
        else:
            send[step - 1][...] = total.astype(jnp.bfloat16)


def split(place, keep, got):
    channels = keep.shape[-1]
    own = jax.ShapeDtypeStruct((2, SLAB, channels), jnp.float32)
    away = jax.ShapeDtypeStruct((2, SLAB, channels), jnp.bfloat16)
    return pl.pallas_call(
        split_kernel,
        out_shape=[own, away, away, away],
        in_specs=[SMEM, VMEM, VMEM],
        out_specs=[VMEM] * 4,
        compiler_params=params(10),
        name="split",
    )(place, keep, got)


def deal_kernel(own_ref, *refs):
    got, out = refs[:3], refs[3]
    total = own_ref[...]
    for piece in got:
        total = total + piece[...].astype(jnp.float32)
    total = total.astype(jnp.bfloat16)
    row = lax.broadcasted_iota(jnp.int32, (PLANE * DEAL, SLAB), 0)
    source = lax.broadcasted_iota(jnp.int32, (PLANE * DEAL, SLAB), 1)
    place = row & (DEAL - 1)
    first = (row >> 4) * SHARE
    dealt = None
    for which in range(2):
        here = place - which * SHARE
        pick = (source == first + here) & (here >= 0) & (here < SHARE)
        part = lax.dot_general(
            jnp.where(pick, 1.0, 0.0).astype(jnp.bfloat16),
            total[which],
            PLAIN,
            preferred_element_type=jnp.float32,
        )
        dealt = part if dealt is None else dealt + part
    out[...] = dealt.astype(jnp.bfloat16).reshape(out.shape)


def deal(*pieces):
    channels = pieces[0].shape[-1]
    return pl.pallas_call(
        deal_kernel,
        out_shape=jax.ShapeDtypeStruct((PLANE, DEAL, channels), jnp.bfloat16),
        in_specs=[VMEM] * 4,
        out_specs=VMEM,
        compiler_params=params(8),
        name="deal",
    )(*pieces)


def last_kernel(got_ref, in_ref, out_ref):
    total = got_ref[0].astype(jnp.float32)
    for source in range(1, PLANE):
        total = total + got_ref[source].astype(jnp.float32)
    in_ref[...] = total[:SHARE]
    out_ref[...] = total[SHARE : 2 * SHARE]


def last(got):
    share = jax.ShapeDtypeStruct((SHARE, got.shape[-1]), jnp.float32)
    return pl.pallas_call(
        last_kernel,
        out_shape=[share, share],
        in_specs=[VMEM],
        out_specs=[VMEM, VMEM],
        compiler_params=params(4),
        name="last",
    )(got)


def along_x(a, step):
    return lax.ppermute(a, "slide", [(i, (i + 4 * step) % 16) for i in range(16)])


def over_plane(a):
    planes = [
        [(4 * x + 2 * y_high + core) * 16 + r for y_high in range(2) for r in range(16)]
        for x in range(4)
        for core in range(2)
    ]
    return lax.all_to_all(a, ("slide", "rep"), 0, 0, tiled=True, axis_index_groups=planes)


def per_device(
    tile_images,
    cotangent,
    depth_kernel,
    depth_bias,
    norm_gain,
    norm_bias,
    expand_weight,
    expand_bias,
    project_weight,
    layer_scale,
    tile_counts,
    send_list,
):
    slide = lax.axis_index("slide").astype(jnp.int32)
    place = (slide >> 2).reshape(1)
    core = (slide & 1).reshape(1)
    slots = send_list.reshape(-1)
    count = tile_counts.reshape(-1)
    conv_weights = (depth_kernel, depth_bias, norm_gain, norm_bias)
    swap = [(i, i ^ 1) for i in range(16)]
    there = lax.ppermute(slots, "slide", swap)
    count_there = lax.ppermute(count, "slide", swap)
    packed = lax.ppermute(pack(slots, tile_images, cotangent), "slide", swap)
    acts, bias = conv_own(
        slots, count, core, tile_images, cotangent, conv_weights, layer_scale, expand_bias
    )
    keep, send = train(
        slots, there, count_there, core, acts, packed, conv_weights, layer_scale, expand_weight,
        bias, project_weight,
    )
    got = lax.ppermute(send, "slide", swap)
    own, *send = split(place, keep, got)
    pieces = [along_x(send[step - 1], step) for step in range(1, 4)]
    return tuple(last(over_plane(deal(own, *pieces))))


def solution(mesh):
    in_specs = (
        P(("slide", "rep"), None, None, None),
        P(("slide", "rep"), None, None, None),
        P(),
        P(),
        P(),
        P(),
        P(),
        P(),
        P(),
        P(),
        P("slide", "rep"),
        P("slide", "rep", None),
    )
    out_specs = (P(("slide", "rep"), None), P(("slide", "rep"), None))
    return jax.shard_map(
        per_device, mesh=mesh, in_specs=in_specs, out_specs=out_specs, check_vma=False
    )
```

```python
import jax
import jax.numpy as jnp
from jax import lax
from jax.experimental import pallas as pl
from jax.experimental.pallas import tpu as pltpu
from jax.sharding import PartitionSpec as P

BANDS = 8
MARGIN = 3
BAND_ROWS = 4
BAND_TOK = 128
SLOTS = 16
GROUP = 2
KEPT = 9
FIRST = 2
ROWS = BAND_ROWS + 2 * MARGIN
HID_STEP = 768
SPAN = GROUP * BAND_TOK
GROUPS = SLOTS // GROUP
PAIRS = 8
CHUNK = 96
PLANE = 16
SHARE = 6
DEAL = 16

root_half = 0.7071067811865476
inv_root_tau = 0.3989422804014327

INNER = (((1,), (1,)), ((), ()))
PLAIN = (((1,), (0,)), ((), ()))


def half_copies(weight_hbm, weight, core, sems):
    copies = []
    for half in range(2):
        for pair in range(PAIRS):
            first = pl.multiple_of((2 * pair + (core ^ half)) * CHUNK, CHUNK)
            copies.append(
                pltpu.make_async_copy(
                    weight_hbm.at[pl.ds(first, CHUNK)],
                    weight.at[pl.ds((half * PAIRS + pair) * CHUNK, CHUNK)],
                    sems.at[half, pair],
                )
            )
    return copies


def pack_list(slots_ref, order_ref):
    listed = jnp.int32(0)
    for slot in range(SLOTS):
        block = slots_ref[slot]
        order_ref[listed] = jnp.maximum(block, 0)
        listed = listed + jnp.where(block >= 0, 1, 0)
    return listed


def block_copies(order_ref, index, images_hbm, cotan_hbm, images, cotans, sems):
    block = order_ref[index]
    tile = block // BANDS
    band = block % BANDS
    first = band * BAND_ROWS
    above = pltpu.make_async_copy(
        images_hbm.at[tile, pl.ds(first - MARGIN, MARGIN)], images.at[pl.ds(0, MARGIN)], sems.at[0]
    )
    middle = pltpu.make_async_copy(
        images_hbm.at[tile, pl.ds(first, BAND_ROWS)], images.at[pl.ds(MARGIN, BAND_ROWS)], sems.at[1]
    )
    below = pltpu.make_async_copy(
        images_hbm.at[tile, pl.ds(first + BAND_ROWS, MARGIN)],
        images.at[pl.ds(MARGIN + BAND_ROWS, MARGIN)],
        sems.at[2],
    )
    error = pltpu.make_async_copy(cotan_hbm.at[tile, pl.ds(first, BAND_ROWS)], cotans, sems.at[3])
    return band, above, middle, below, error


def start_block(band, above, middle, below, error):
    pl.when(band > 0)(above.start)
    middle.start()
    pl.when(band < BANDS - 1)(below.start)
    error.start()


def conv_norm(image, band, taps, conv_out, depth_bias, gain, norm_bias):
    _, side, channels = image.shape

    @pl.when(band == 0)
    def _():
        image[:MARGIN] = jnp.zeros((MARGIN, side, channels), image.dtype)

    @pl.when(band == BANDS - 1)
    def _():
        image[MARGIN + BAND_ROWS : ROWS] = jnp.zeros((MARGIN, side, channels), image.dtype)

    column = lax.broadcasted_iota(jnp.int32, (8, 128), 0)
    for lanes in range(0, channels, 128):
        part = slice(lanes, lanes + 128)
        for row in range(BAND_ROWS):
            sums = [None] * 7
            for dy in range(7):
                x = image[row + dy, :, part].astype(jnp.float32)
                for dx in range(7):
                    term = x * taps[dy, dx : dx + 1, part]
                    sums[dx] = term if sums[dx] is None else sums[dx] + term
            total = sums[MARGIN] + depth_bias[:, part]
            for dx in range(-MARGIN, MARGIN + 1):
                if dx != 0:
                    moved = pltpu.roll(sums[dx + MARGIN], (-dx) % side, 0)
                    if dx < 0:
                        edge = jnp.where(column + dx >= 0, moved[:8], 0.0)
                        moved = jnp.concatenate([edge, moved[8:]], axis=0)
                    else:
                        edge = jnp.where(column + dx < 8, moved[side - 8 :], 0.0)
                        moved = jnp.concatenate([moved[: side - 8], edge], axis=0)
                    total = total + moved
            conv_out[row * side : (row + 1) * side, part] = total
    mixed = conv_out[...]
    centre = jnp.mean(mixed, axis=-1, keepdims=True)
    away = mixed - centre
    spread = jnp.mean(away * away, axis=-1, keepdims=True)
    return (away * lax.rsqrt(spread + 1e-06) * gain + norm_bias).astype(jnp.bfloat16)


def scale_errors(errors, scale):
    rows, side, channels = errors.shape
    flat = errors[...].reshape(rows * side, channels)
    return (flat.astype(jnp.float32) * scale).astype(jnp.bfloat16)


def conv_blocks(low, high, refs, between):
    (
        count_ref,
        images_hbm,
        cotan_hbm,
        taps_ref,
        depth_bias_ref,
        gain_ref,
        norm_bias_ref,
        scale_ref,
        acts_hbm,
        images,
        cotans,
        taps,
        acts,
        conv_out,
        order_ref,
        image_sems,
        acts_sems,
    ) = refs
    channels = images_hbm.shape[3]

    def copies(index):
        return block_copies(
            order_ref,
            index,
            images_hbm,
            cotan_hbm,
            images.at[index - low],
            cotans.at[index - low],
            image_sems.at[index - low],
        )

    @pl.loop(low, high)
    def _(index):
        start_block(*copies(index))

    taps[...] = taps_ref[...].astype(jnp.float32)
    depth_bias = depth_bias_ref[...].reshape(1, channels)
    gain = gain_ref[...].reshape(1, channels)
    norm_bias = norm_bias_ref[...].reshape(1, channels)
    scale = scale_ref[...].reshape(1, channels) / count_ref[0].astype(jnp.float32)

    def acts_copy(index):
        rows = pl.ds(pl.multiple_of((index - low) * BAND_TOK, BAND_TOK), BAND_TOK)
        return pltpu.make_async_copy(
            acts.at[:, rows], acts_hbm.at[:, rows], acts_sems.at[index - low]
        )

    @pl.loop(low, high)
    def _(index):
        band, above, middle, below, error = copies(index)
        pl.when(band > 0)(above.wait)
        middle.wait()
        pl.when(band < BANDS - 1)(below.wait)
        rows = pl.ds(pl.multiple_of((index - low) * BAND_TOK, BAND_TOK), BAND_TOK)
        acts[0, rows, :] = conv_norm(
            images.at[index - low], band, taps, conv_out, depth_bias, gain, norm_bias
        )
        error.wait()
        acts[1, rows, :] = scale_errors(cotans.at[index - low], scale)
        acts_copy(index).start()
        if between is not None:
            pl.when(index == low)(between)

    @pl.loop(low, high)
    def _(index):
        acts_copy(index).wait()


def first_kernel(slots_ref, *refs):
    (packed_hbm, acts_hbm), packed, (sems, out_sems) = refs[8:10], refs[15], refs[19:]
    refs = refs[:8] + (acts_hbm,) + refs[10:15] + refs[16:19]
    images_hbm, cotan_hbm, order_ref = refs[1], refs[2], refs[14]
    listed = pack_list(slots_ref, order_ref)

    def copies(index):
        place = packed.at[index - KEPT]
        return block_copies(
            order_ref,
            index,
            images_hbm,
            cotan_hbm,
            place.at[pl.ds(0, ROWS)],
            place.at[pl.ds(ROWS, BAND_ROWS)],
            sems.at[index - KEPT],
        )

    def out_copy(index):
        place = index - KEPT
        return pltpu.make_async_copy(packed.at[place], packed_hbm.at[place], out_sems.at[place])

    @pl.loop(KEPT, listed)
    def _(index):
        start_block(*copies(index))

    def send_out():
        @pl.loop(KEPT, listed)
        def _(index):
            band, above, middle, below, error = copies(index)
            pl.when(band > 0)(above.wait)
            middle.wait()
            pl.when(band < BANDS - 1)(below.wait)
            error.wait()
            out_copy(index).start()

    conv_blocks(0, jnp.minimum(listed, FIRST), refs, send_out)

    @pl.loop(KEPT, listed)
    def _(index):
        out_copy(index).wait()


def other_kernel(slots_ref, *refs):
    listed = pack_list(slots_ref, refs[14])
    conv_blocks(FIRST, jnp.maximum(jnp.minimum(listed, KEPT), FIRST), refs, None)


def train_kernel(
    slots_ref,
    there_ref,
    count_there_ref,
    core_ref,
    first_hbm,
    other_hbm,
    packed_hbm,
    taps_ref,
    depth_bias_ref,
    gain_ref,
    norm_bias_ref,
    scale_ref,
    expand_hbm,
    expand_bias_ref,
    project_hbm,
    keep_hbm,
    send_hbm,
    packed,
    taps,
    acts,
    conv_out,
    expand,
    project,
    grad,
    bias_all,
    bias_ref,
    out,
    order_ref,
    packed_sems,
    acts_sems,
    weight_sems,
    out_sems,
):
    channels = packed_hbm.shape[3]
    core = core_ref[0]
    listed_there = pack_list(there_ref, order_ref)
    listed = jnp.int32(0)
    for slot in range(SLOTS):
        listed = listed + jnp.where(slots_ref[slot] >= 0, 1, 0)
    own = jnp.minimum(listed, KEPT)
    taken = jnp.maximum(listed_there - KEPT, 0)

    def packed_copy(place):
        return pltpu.make_async_copy(packed_hbm.at[place], packed.at[place], packed_sems.at[place])

    def acts_copy(source, low, index):
        rows = pl.ds(pl.multiple_of((index - low) * BAND_TOK, BAND_TOK), BAND_TOK)
        there = pl.ds(pl.multiple_of(index * BAND_TOK, BAND_TOK), BAND_TOK)
        return pltpu.make_async_copy(source.at[:, rows], acts.at[:, there], acts_sems.at[index])

    @pl.loop(0, taken)
    def _(index):
        packed_copy(index).start()

    weight_copies = half_copies(expand_hbm, expand, core, weight_sems.at[0])
    weight_copies += half_copies(project_hbm, project, core, weight_sems.at[1])
    for copy in weight_copies:
        copy.start()

    early = jnp.minimum(own, FIRST)

    @pl.loop(0, early)
    def _(index):
        acts_copy(first_hbm, 0, index).start()

    @pl.loop(FIRST, own)
    def _(index):
        acts_copy(other_hbm, FIRST, index).start()

    hidden = expand_bias_ref.shape[0]
    for first in range(0, hidden, 128):
        row = expand_bias_ref[pl.ds(first, 128)].reshape(1, 128)
        bias_all[pl.ds(first, 128), :] = jnp.broadcast_to(row, (128, 128)).T
    for half in range(2):
        for pair in range(PAIRS):
            rows = pl.ds(pl.multiple_of((2 * pair + (core ^ half)) * CHUNK, CHUNK), CHUNK)
            bias_ref[pl.ds((half * PAIRS + pair) * CHUNK, CHUNK), :] = bias_all[rows, :]
    taps[...] = taps_ref[...].astype(jnp.float32)
    depth_bias = depth_bias_ref[...].reshape(1, channels)
    gain = gain_ref[...].reshape(1, channels)
    norm_bias = norm_bias_ref[...].reshape(1, channels)
    scale = scale_ref[...].reshape(1, channels) / count_there_ref[0].astype(jnp.float32)
    grad[...] = jnp.zeros(grad.shape, jnp.float32)

    @pl.loop(0, taken)
    def _(index):
        packed_copy(index).wait()
        rows = pl.ds(pl.multiple_of((own + index) * BAND_TOK, BAND_TOK), BAND_TOK)
        band = order_ref[KEPT + index] % BANDS
        acts[0, rows, :] = conv_norm(
            packed.at[index, pl.ds(0, ROWS)], band, taps, conv_out, depth_bias, gain, norm_bias
        )
        acts[1, rows, :] = scale_errors(packed.at[index, pl.ds(ROWS, BAND_ROWS)], scale)

    total = own + taken

    @pl.when(total % GROUP != 0)
    def _():
        rows = pl.ds(pl.multiple_of(total * BAND_TOK, BAND_TOK), BAND_TOK)
        acts[:, rows, :] = jnp.zeros((2, BAND_TOK, channels), acts.dtype)

    for copy in weight_copies:
        copy.wait()

    @pl.loop(0, early)
    def _(index):
        acts_copy(first_hbm, 0, index).wait()

    @pl.loop(FIRST, own)
    def _(index):
        acts_copy(other_hbm, FIRST, index).wait()

    half = hidden // 2

    @pl.loop(0, (total + GROUP - 1) // GROUP)
    def _(group):
        rows = pl.ds(pl.multiple_of(group * SPAN, SPAN), SPAN)
        flat_in = acts[0, rows, :]
        flat_err = acts[1, rows, :]
        for start in range(0, 2 * half, HID_STEP):
            units = slice(start, start + HID_STEP)
            pre_act = lax.dot_general(
                expand[units, :], flat_in, INNER, preferred_element_type=jnp.float32
            )
            back_grad = lax.dot_general(
                project[units, :], flat_err, INNER, preferred_element_type=jnp.float32
            )
            pre_act = pre_act + jnp.concatenate([bias_ref[units, :]] * (SPAN // 128), axis=1)
            share = 0.5 * (1.0 + lax.erf(pre_act * root_half))
            activated = (pre_act * share).astype(jnp.bfloat16)
            bell = jnp.exp(-0.5 * pre_act * pre_act) * inv_root_tau
            slope_term = (back_grad * (share + pre_act * bell)).astype(jnp.bfloat16)
            grad[0, units, :] += lax.dot_general(
                slope_term, flat_in, PLAIN, preferred_element_type=jnp.float32
            )
            grad[1, units, :] += lax.dot_general(
                activated, flat_err, PLAIN, preferred_element_type=jnp.float32
            )

    def out_copy(half, pair):
        return pltpu.make_async_copy(
            out.at[half, pair], (keep_hbm, send_hbm)[half].at[pair], out_sems.at[half, pair]
        )

    for half in (1, 0):
        for pair in range(PAIRS):
            rows = slice((half * PAIRS + pair) * CHUNK, (half * PAIRS + pair + 1) * CHUNK)
            out[half, pair] = grad[:, rows, :].astype(out.dtype)
            out_copy(half, pair).start()
    for half in (1, 0):
        for pair in range(PAIRS):
            out_copy(half, pair).wait()


SMEM = pl.BlockSpec(memory_space=pltpu.SMEM)
VMEM = pl.BlockSpec(memory_space=pltpu.VMEM)
HBM = pl.BlockSpec(memory_space=pl.ANY)


def params(mib):
    return pltpu.CompilerParams(vmem_limit_bytes=mib * 2**20)


def conv_scratch(blocks, side, channels):
    bf16, f32 = jnp.bfloat16, jnp.float32
    return [
        pltpu.VMEM((blocks, ROWS, side, channels), bf16),
        pltpu.VMEM((blocks, BAND_ROWS, side, channels), bf16),
        pltpu.VMEM((7, 7, channels), f32),
        pltpu.VMEM((2, blocks * BAND_TOK, channels), bf16),
        pltpu.VMEM((BAND_TOK, channels), f32),
    ]


def conv_first(slots, count, tile_images, cotangent, conv_weights, scale):
    side, channels = tile_images.shape[1], tile_images.shape[3]
    packed = (SLOTS - KEPT, ROWS + BAND_ROWS, side, channels)
    return pl.pallas_call(
        first_kernel,
        out_shape=(
            jax.ShapeDtypeStruct(packed, jnp.bfloat16),
            jax.ShapeDtypeStruct((2, FIRST * BAND_TOK, channels), jnp.bfloat16),
        ),
        in_specs=[SMEM] * 2 + [HBM] * 2 + [VMEM] * 5,
        out_specs=[HBM] * 2,
        scratch_shapes=conv_scratch(FIRST, side, channels)
        + [
            pltpu.VMEM(packed, jnp.bfloat16),
            pltpu.SMEM((SLOTS + 1,), jnp.int32),
            pltpu.SemaphoreType.DMA((FIRST, 4)),
            pltpu.SemaphoreType.DMA((FIRST,)),
            pltpu.SemaphoreType.DMA((SLOTS - KEPT, 4)),
            pltpu.SemaphoreType.DMA((SLOTS - KEPT,)),
        ],
        compiler_params=params(56),
        name="conv_first",
    )(slots, count, tile_images, cotangent, *conv_weights, scale)


def conv_other(slots, count, tile_images, cotangent, conv_weights, scale):
    side, channels = tile_images.shape[1], tile_images.shape[3]
    blocks = KEPT - FIRST
    return pl.pallas_call(
        other_kernel,
        out_shape=jax.ShapeDtypeStruct((2, blocks * BAND_TOK, channels), jnp.bfloat16),
        in_specs=[SMEM] * 2 + [HBM] * 2 + [VMEM] * 5,
        out_specs=HBM,
        scratch_shapes=conv_scratch(blocks, side, channels)
        + [
            pltpu.SMEM((SLOTS + 1,), jnp.int32),
            pltpu.SemaphoreType.DMA((blocks, 4)),
            pltpu.SemaphoreType.DMA((blocks,)),
        ],
        compiler_params=params(56),
        cost_estimate=pl.CostEstimate(flops=8 * 10**9, bytes_accessed=10**7, transcendentals=0),
        name="conv_other",
    )(slots, count, tile_images, cotangent, *conv_weights, scale)


def train(
    slots, there, count_there, core, acts, packed, conv_weights, scale, expand_weight, expand_bias,
    project_weight,
):
    hidden, channels = expand_weight.shape
    bf16, f32 = jnp.bfloat16, jnp.float32
    return pl.pallas_call(
        train_kernel,
        out_shape=[jax.ShapeDtypeStruct((PAIRS, 2, CHUNK, channels), bf16)] * 2,
        in_specs=[SMEM] * 4 + [HBM] * 3 + [VMEM] * 5 + [HBM, VMEM, HBM],
        out_specs=[HBM, HBM],
        scratch_shapes=[
            pltpu.VMEM(packed.shape, bf16),
            pltpu.VMEM((7, 7, channels), f32),
            pltpu.VMEM((2, SLOTS * BAND_TOK, channels), bf16),
            pltpu.VMEM((BAND_TOK, channels), f32),
            pltpu.VMEM((hidden, channels), bf16),
            pltpu.VMEM((hidden, channels), bf16),
            pltpu.VMEM((2, hidden, channels), f32),
            pltpu.VMEM((hidden, 128), f32),
            pltpu.VMEM((hidden, 128), f32),
            pltpu.VMEM((2, PAIRS, 2, CHUNK, channels), bf16),
            pltpu.SMEM((SLOTS + 1,), jnp.int32),
            pltpu.SemaphoreType.DMA((SLOTS - KEPT,)),
            pltpu.SemaphoreType.DMA((SLOTS,)),
            pltpu.SemaphoreType.DMA((2, 2, PAIRS)),
            pltpu.SemaphoreType.DMA((2, PAIRS)),
        ],
        compiler_params=params(56),
        cost_estimate=pl.CostEstimate(flops=9 * 10**9, bytes_accessed=10**7, transcendentals=0),
        name="train",
    )(
        slots, there, count_there, core, *acts, packed, *conv_weights, scale, expand_weight,
        expand_bias, project_weight,
    )


def deal_kernel(got_ref, out):
    total = got_ref[0].astype(jnp.float32)
    for source in range(1, PAIRS):
        total = total + got_ref[source].astype(jnp.float32)
    total = total.astype(jnp.bfloat16)
    row = lax.broadcasted_iota(jnp.int32, (PLANE * DEAL, CHUNK), 0)
    source = lax.broadcasted_iota(jnp.int32, (PLANE * DEAL, CHUNK), 1)
    place = row & (DEAL - 1)
    first = (row >> 4) * SHARE
    dealt = None
    for which in range(2):
        here = place - which * SHARE
        pick = (source == first + here) & (here >= 0) & (here < SHARE)
        part = lax.dot_general(
            jnp.where(pick, 1.0, 0.0).astype(jnp.bfloat16),
            total[which],
            PLAIN,
            preferred_element_type=jnp.float32,
        )
        dealt = part if dealt is None else dealt + part
    out[...] = dealt.astype(jnp.bfloat16).reshape(out.shape)


def deal(got):
    channels = got.shape[-1]
    return pl.pallas_call(
        deal_kernel,
        out_shape=jax.ShapeDtypeStruct((PLANE, DEAL, channels), jnp.bfloat16),
        in_specs=[VMEM],
        out_specs=VMEM,
        compiler_params=params(8),
        name="deal",
    )(got)


def last_kernel(got_ref, in_ref, out_ref):
    total = got_ref[0].astype(jnp.float32)
    for source in range(1, PLANE):
        total = total + got_ref[source].astype(jnp.float32)
    in_ref[...] = total[:SHARE]
    out_ref[...] = total[SHARE : 2 * SHARE]


def last(got):
    share = jax.ShapeDtypeStruct((SHARE, got.shape[-1]), jnp.float32)
    return pl.pallas_call(
        last_kernel,
        out_shape=[share, share],
        in_specs=[VMEM],
        out_specs=[VMEM, VMEM],
        compiler_params=params(4),
        name="last",
    )(got)


def over_chips(a):
    cores = [[place + core for place in range(0, SLOTS, 2)] for core in range(2)]
    return lax.all_to_all(a, "slide", 0, 0, tiled=True, axis_index_groups=cores)


def per_device(
    tile_images,
    cotangent,
    depth_kernel,
    depth_bias,
    norm_gain,
    norm_bias,
    expand_weight,
    expand_bias,
    project_weight,
    layer_scale,
    tile_counts,
    send_list,
):
    slide = lax.axis_index("slide").astype(jnp.int32)
    core = (slide & 1).reshape(1)
    slots = send_list.reshape(-1)
    count = tile_counts.reshape(-1)
    conv_weights = (depth_kernel, depth_bias, norm_gain, norm_bias)
    swap = [(i, i ^ 1) for i in range(16)]
    there = lax.ppermute(slots, "slide", swap)
    count_there = lax.ppermute(count, "slide", swap)
    packed, first = conv_first(
        slots, count, tile_images, cotangent, conv_weights, layer_scale
    )
    packed = lax.ppermute(packed, "slide", swap)
    other = conv_other(slots, count, tile_images, cotangent, conv_weights, layer_scale)
    keep, send = train(
        slots, there, count_there, core, (first, other), packed, conv_weights, layer_scale,
        expand_weight, expand_bias, project_weight,
    )
    got = lax.ppermute(send, "slide", swap)
    both = (keep.astype(jnp.float32) + got.astype(jnp.float32)).astype(jnp.bfloat16)
    got = deal(over_chips(both))
    return tuple(last(lax.all_to_all(got, "rep", 0, 0, tiled=True)))


def solution(mesh):
    in_specs = (
        P(("slide", "rep"), None, None, None),
        P(("slide", "rep"), None, None, None),
        P(),
        P(),
        P(),
        P(),
        P(),
        P(),
        P(),
        P(),
        P("slide", "rep"),
        P("slide", "rep", None),
    )
    out_specs = (P(("slide", "rep"), None), P(("slide", "rep"), None))
    return jax.shard_map(
        per_device, mesh=mesh, in_specs=in_specs, out_specs=out_specs, check_vma=False
    )
```

```python
import jax
import jax.numpy as jnp
from jax import lax
from jax.experimental import pallas as pl
from jax.experimental.pallas import tpu as pltpu
from jax.sharding import PartitionSpec as P

BANDS = 8
MARGIN = 3
BAND_ROWS = 4
BAND_TOK = 128
SLOTS = 16
GROUP = 2
KEPT = 9
FIRST = 2
ROWS = BAND_ROWS + 2 * MARGIN
HID_STEP = 1536
SPAN = GROUP * BAND_TOK
GROUPS = SLOTS // GROUP
PAIRS = 8
CHUNK = 96
PLANE = 16
SHARE = 6
DEAL = 16

root_half = 0.7071067811865476
inv_root_tau = 0.3989422804014327

INNER = (((1,), (1,)), ((), ()))
PLAIN = (((1,), (0,)), ((), ()))


def half_copies(weight_hbm, weight, core, sems):
    copies = []
    for half in range(2):
        for pair in range(PAIRS):
            first = pl.multiple_of((2 * pair + (core ^ half)) * CHUNK, CHUNK)
            copies.append(
                pltpu.make_async_copy(
                    weight_hbm.at[pl.ds(first, CHUNK)],
                    weight.at[pl.ds((half * PAIRS + pair) * CHUNK, CHUNK)],
                    sems.at[half, pair],
                )
            )
    return copies


def pack_list(slots_ref, order_ref):
    listed = jnp.int32(0)
    for slot in range(SLOTS):
        block = slots_ref[slot]
        order_ref[listed] = jnp.maximum(block, 0)
        listed = listed + jnp.where(block >= 0, 1, 0)
    return listed


def block_copies(order_ref, index, images_hbm, cotan_hbm, images, cotans, sems):
    block = order_ref[index]
    tile = block // BANDS
    band = block % BANDS
    first = band * BAND_ROWS
    above = pltpu.make_async_copy(
        images_hbm.at[tile, pl.ds(first - MARGIN, MARGIN)], images.at[pl.ds(0, MARGIN)], sems.at[0]
    )
    middle = pltpu.make_async_copy(
        images_hbm.at[tile, pl.ds(first, BAND_ROWS)], images.at[pl.ds(MARGIN, BAND_ROWS)], sems.at[1]
    )
    below = pltpu.make_async_copy(
        images_hbm.at[tile, pl.ds(first + BAND_ROWS, MARGIN)],
        images.at[pl.ds(MARGIN + BAND_ROWS, MARGIN)],
        sems.at[2],
    )
    error = pltpu.make_async_copy(cotan_hbm.at[tile, pl.ds(first, BAND_ROWS)], cotans, sems.at[3])
    return band, above, middle, below, error


def start_block(band, above, middle, below, error):
    pl.when(band > 0)(above.start)
    middle.start()
    pl.when(band < BANDS - 1)(below.start)
    error.start()


def conv_norm(image, band, taps, conv_out, depth_bias, gain, norm_bias):
    _, side, channels = image.shape

    @pl.when(band == 0)
    def _():
        image[:MARGIN] = jnp.zeros((MARGIN, side, channels), image.dtype)

    @pl.when(band == BANDS - 1)
    def _():
        image[MARGIN + BAND_ROWS : ROWS] = jnp.zeros((MARGIN, side, channels), image.dtype)

    column = lax.broadcasted_iota(jnp.int32, (8, 128), 0)
    for lanes in range(0, channels, 128):
        part = slice(lanes, lanes + 128)
        flat = image[:, :, part].astype(jnp.float32)
        for row in range(BAND_ROWS):
            sums = [None] * 7
            for dy in range(7):
                x = flat[row + dy]
                for dx in range(7):
                    term = x * taps[dy, dx : dx + 1, part]
                    sums[dx] = term if sums[dx] is None else sums[dx] + term
            total = sums[MARGIN] + depth_bias[:, part]
            for dx in range(-MARGIN, MARGIN + 1):
                if dx != 0:
                    moved = pltpu.roll(sums[dx + MARGIN], (-dx) % side, 0)
                    if dx < 0:
                        edge = jnp.where(column + dx >= 0, moved[:8], 0.0)
                        moved = jnp.concatenate([edge, moved[8:]], axis=0)
                    else:
                        edge = jnp.where(column + dx < 8, moved[side - 8 :], 0.0)
                        moved = jnp.concatenate([moved[: side - 8], edge], axis=0)
                    total = total + moved
            conv_out[row * side : (row + 1) * side, part] = total
    mixed = conv_out[...]
    centre = jnp.mean(mixed, axis=-1, keepdims=True)
    away = mixed - centre
    spread = jnp.mean(away * away, axis=-1, keepdims=True)
    return (away * lax.rsqrt(spread + 1e-06) * gain + norm_bias).astype(jnp.bfloat16)


def scale_errors(errors, scale):
    rows, side, channels = errors.shape
    flat = errors[...].reshape(rows * side, channels)
    return (flat.astype(jnp.float32) * scale).astype(jnp.bfloat16)


def conv_blocks(low, high, refs, between):
    (
        count_ref,
        images_hbm,
        cotan_hbm,
        taps_ref,
        depth_bias_ref,
        gain_ref,
        norm_bias_ref,
        scale_ref,
        acts_hbm,
        images,
        cotans,
        taps,
        acts,
        conv_out,
        order_ref,
        image_sems,
        acts_sems,
    ) = refs
    channels = images_hbm.shape[3]

    def copies(index):
        return block_copies(
            order_ref,
            index,
            images_hbm,
            cotan_hbm,
            images.at[index - low],
            cotans.at[index - low],
            image_sems.at[index - low],
        )

    @pl.loop(low, high)
    def _(index):
        start_block(*copies(index))

    taps[...] = taps_ref[...].astype(jnp.float32)
    depth_bias = depth_bias_ref[...].reshape(1, channels)
    gain = gain_ref[...].reshape(1, channels)
    norm_bias = norm_bias_ref[...].reshape(1, channels)
    scale = scale_ref[...].reshape(1, channels) / count_ref[0].astype(jnp.float32)

    def acts_copy(index):
        rows = pl.ds(pl.multiple_of((index - low) * BAND_TOK, BAND_TOK), BAND_TOK)
        return pltpu.make_async_copy(
            acts.at[:, rows], acts_hbm.at[:, rows], acts_sems.at[index - low]
        )

    @pl.loop(low, high)
    def _(index):
        band, above, middle, below, error = copies(index)
        pl.when(band > 0)(above.wait)
        middle.wait()
        pl.when(band < BANDS - 1)(below.wait)
        rows = pl.ds(pl.multiple_of((index - low) * BAND_TOK, BAND_TOK), BAND_TOK)
        acts[0, rows, :] = conv_norm(
            images.at[index - low], band, taps, conv_out, depth_bias, gain, norm_bias
        )
        error.wait()
        acts[1, rows, :] = scale_errors(cotans.at[index - low], scale)
        acts_copy(index).start()
        if between is not None:
            pl.when(index == low)(between)

    @pl.loop(low, high)
    def _(index):
        acts_copy(index).wait()


def first_kernel(slots_ref, *refs):
    (packed_hbm, acts_hbm), packed, (sems, out_sems) = refs[8:10], refs[15], refs[19:]
    refs = refs[:8] + (acts_hbm,) + refs[10:15] + refs[16:19]
    images_hbm, cotan_hbm, order_ref = refs[1], refs[2], refs[14]
    listed = pack_list(slots_ref, order_ref)

    def copies(index):
        place = packed.at[index - KEPT]
        return block_copies(
            order_ref,
            index,
            images_hbm,
            cotan_hbm,
            place.at[pl.ds(0, ROWS)],
            place.at[pl.ds(ROWS, BAND_ROWS)],
            sems.at[index - KEPT],
        )

    def out_copy(index):
        place = index - KEPT
        return pltpu.make_async_copy(packed.at[place], packed_hbm.at[place], out_sems.at[place])

    @pl.loop(KEPT, listed)
    def _(index):
        start_block(*copies(index))

    def send_out():
        @pl.loop(KEPT, listed)
        def _(index):
            band, above, middle, below, error = copies(index)
            pl.when(band > 0)(above.wait)
            middle.wait()
            pl.when(band < BANDS - 1)(below.wait)
            error.wait()
            out_copy(index).start()

    conv_blocks(0, jnp.minimum(listed, FIRST), refs, send_out)

    @pl.loop(KEPT, listed)
    def _(index):
        out_copy(index).wait()


def other_kernel(slots_ref, *refs):
    listed = pack_list(slots_ref, refs[14])
    conv_blocks(FIRST, jnp.maximum(jnp.minimum(listed, KEPT), FIRST), refs, None)


def train_kernel(
    slots_ref,
    there_ref,
    count_there_ref,
    core_ref,
    first_hbm,
    other_hbm,
    packed_hbm,
    taps_ref,
    depth_bias_ref,
    gain_ref,
    norm_bias_ref,
    scale_ref,
    expand_hbm,
    expand_bias_ref,
    project_hbm,
    keep_hbm,
    send_hbm,
    packed,
    taps,
    acts,
    conv_out,
    expand,
    project,
    grad,
    bias_all,
    bias_ref,
    out,
    order_ref,
    packed_sems,
    acts_sems,
    weight_sems,
    out_sems,
):
    channels = packed_hbm.shape[3]
    core = core_ref[0]
    listed_there = pack_list(there_ref, order_ref)
    listed = jnp.int32(0)
    for slot in range(SLOTS):
        listed = listed + jnp.where(slots_ref[slot] >= 0, 1, 0)
    own = jnp.minimum(listed, KEPT)
    taken = jnp.maximum(listed_there - KEPT, 0)

    def packed_copy(place):
        return pltpu.make_async_copy(packed_hbm.at[place], packed.at[place], packed_sems.at[place])

    def acts_copy(source, low, index):
        rows = pl.ds(pl.multiple_of((index - low) * BAND_TOK, BAND_TOK), BAND_TOK)
        there = pl.ds(pl.multiple_of(index * BAND_TOK, BAND_TOK), BAND_TOK)
        return pltpu.make_async_copy(source.at[:, rows], acts.at[:, there], acts_sems.at[index])

    @pl.loop(0, taken)
    def _(index):
        packed_copy(index).start()

    weight_copies = half_copies(expand_hbm, expand, core, weight_sems.at[0])
    weight_copies += half_copies(project_hbm, project, core, weight_sems.at[1])
    for copy in weight_copies:
        copy.start()

    early = jnp.minimum(own, FIRST)

    @pl.loop(0, early)
    def _(index):
        acts_copy(first_hbm, 0, index).start()

    @pl.loop(FIRST, own)
    def _(index):
        acts_copy(other_hbm, FIRST, index).start()

    hidden = expand_bias_ref.shape[0]
    for first in range(0, hidden, 128):
        row = expand_bias_ref[pl.ds(first, 128)].reshape(1, 128)
        bias_all[pl.ds(first, 128), :] = jnp.broadcast_to(row, (128, 128)).T
    for half in range(2):
        for pair in range(PAIRS):
            rows = pl.ds(pl.multiple_of((2 * pair + (core ^ half)) * CHUNK, CHUNK), CHUNK)
            bias_ref[pl.ds((half * PAIRS + pair) * CHUNK, CHUNK), :] = bias_all[rows, :]
    taps[...] = taps_ref[...].astype(jnp.float32)
    depth_bias = depth_bias_ref[...].reshape(1, channels)
    gain = gain_ref[...].reshape(1, channels)
    norm_bias = norm_bias_ref[...].reshape(1, channels)
    scale = scale_ref[...].reshape(1, channels) / count_there_ref[0].astype(jnp.float32)
    grad[...] = jnp.zeros(grad.shape, jnp.float32)

    @pl.loop(0, taken)
    def _(index):
        packed_copy(index).wait()
        rows = pl.ds(pl.multiple_of((own + index) * BAND_TOK, BAND_TOK), BAND_TOK)
        band = order_ref[KEPT + index] % BANDS
        acts[0, rows, :] = conv_norm(
            packed.at[index, pl.ds(0, ROWS)], band, taps, conv_out, depth_bias, gain, norm_bias
        )
        acts[1, rows, :] = scale_errors(packed.at[index, pl.ds(ROWS, BAND_ROWS)], scale)

    total = own + taken

    @pl.when(total % GROUP != 0)
    def _():
        rows = pl.ds(pl.multiple_of(total * BAND_TOK, BAND_TOK), BAND_TOK)
        acts[:, rows, :] = jnp.zeros((2, BAND_TOK, channels), acts.dtype)

    for copy in weight_copies:
        copy.wait()

    @pl.loop(0, early)
    def _(index):
        acts_copy(first_hbm, 0, index).wait()

    @pl.loop(FIRST, own)
    def _(index):
        acts_copy(other_hbm, FIRST, index).wait()

    half = hidden // 2

    @pl.loop(0, (total + GROUP - 1) // GROUP)
    def _(group):
        rows = pl.ds(pl.multiple_of(group * SPAN, SPAN), SPAN)
        flat_in = acts[0, rows, :]
        flat_err = acts[1, rows, :]
        for start in range(0, 2 * half, HID_STEP):
            units = slice(start, start + HID_STEP)
            pre_act = lax.dot_general(
                expand[units, :], flat_in, INNER, preferred_element_type=jnp.float32
            )
            back_grad = lax.dot_general(
                project[units, :], flat_err, INNER, preferred_element_type=jnp.float32
            )
            pre_act = pre_act + jnp.concatenate([bias_ref[units, :]] * (SPAN // 128), axis=1)
            share = 0.5 * (1.0 + lax.erf(pre_act * root_half))
            activated = (pre_act * share).astype(jnp.bfloat16)
            bell = jnp.exp(-0.5 * pre_act * pre_act) * inv_root_tau
            slope_term = (back_grad * (share + pre_act * bell)).astype(jnp.bfloat16)
            grad[0, units, :] += lax.dot_general(
                slope_term, flat_in, PLAIN, preferred_element_type=jnp.float32
            )
            grad[1, units, :] += lax.dot_general(
                activated, flat_err, PLAIN, preferred_element_type=jnp.float32
            )

    def out_copy(half, pair):
        return pltpu.make_async_copy(
            out.at[half, pair], (keep_hbm, send_hbm)[half].at[pair], out_sems.at[half, pair]
        )

    for half in (1, 0):
        for pair in range(PAIRS):
            rows = slice((half * PAIRS + pair) * CHUNK, (half * PAIRS + pair + 1) * CHUNK)
            out[half, pair] = grad[:, rows, :].astype(out.dtype)
            out_copy(half, pair).start()
    for half in (1, 0):
        for pair in range(PAIRS):
            out_copy(half, pair).wait()


SMEM = pl.BlockSpec(memory_space=pltpu.SMEM)
VMEM = pl.BlockSpec(memory_space=pltpu.VMEM)
HBM = pl.BlockSpec(memory_space=pl.ANY)


def params(mib):
    return pltpu.CompilerParams(vmem_limit_bytes=mib * 2**20)


def conv_scratch(blocks, side, channels):
    bf16, f32 = jnp.bfloat16, jnp.float32
    return [
        pltpu.VMEM((blocks, ROWS, side, channels), bf16),
        pltpu.VMEM((blocks, BAND_ROWS, side, channels), bf16),
        pltpu.VMEM((7, 7, channels), f32),
        pltpu.VMEM((2, blocks * BAND_TOK, channels), bf16),
        pltpu.VMEM((BAND_TOK, channels), f32),
    ]


def conv_first(slots, count, tile_images, cotangent, conv_weights, scale):
    side, channels = tile_images.shape[1], tile_images.shape[3]
    packed = (SLOTS - KEPT, ROWS + BAND_ROWS, side, channels)
    return pl.pallas_call(
        first_kernel,
        out_shape=(
            jax.ShapeDtypeStruct(packed, jnp.bfloat16),
            jax.ShapeDtypeStruct((2, FIRST * BAND_TOK, channels), jnp.bfloat16),
        ),
        in_specs=[SMEM] * 2 + [HBM] * 2 + [VMEM] * 5,
        out_specs=[HBM] * 2,
        scratch_shapes=conv_scratch(FIRST, side, channels)
        + [
            pltpu.VMEM(packed, jnp.bfloat16),
            pltpu.SMEM((SLOTS + 1,), jnp.int32),
            pltpu.SemaphoreType.DMA((FIRST, 4)),
            pltpu.SemaphoreType.DMA((FIRST,)),
            pltpu.SemaphoreType.DMA((SLOTS - KEPT, 4)),
            pltpu.SemaphoreType.DMA((SLOTS - KEPT,)),
        ],
        compiler_params=params(56),
        name="conv_first",
    )(slots, count, tile_images, cotangent, *conv_weights, scale)


def conv_other(slots, count, tile_images, cotangent, conv_weights, scale):
    side, channels = tile_images.shape[1], tile_images.shape[3]
    blocks = KEPT - FIRST
    return pl.pallas_call(
        other_kernel,
        out_shape=jax.ShapeDtypeStruct((2, blocks * BAND_TOK, channels), jnp.bfloat16),
        in_specs=[SMEM] * 2 + [HBM] * 2 + [VMEM] * 5,
        out_specs=HBM,
        scratch_shapes=conv_scratch(blocks, side, channels)
        + [
            pltpu.SMEM((SLOTS + 1,), jnp.int32),
            pltpu.SemaphoreType.DMA((blocks, 4)),
            pltpu.SemaphoreType.DMA((blocks,)),
        ],
        compiler_params=params(62),
        cost_estimate=pl.CostEstimate(flops=8 * 10**9, bytes_accessed=10**7, transcendentals=0),
        name="conv_other",
    )(slots, count, tile_images, cotangent, *conv_weights, scale)


def train(
    slots, there, count_there, core, acts, packed, conv_weights, scale, expand_weight, expand_bias,
    project_weight,
):
    hidden, channels = expand_weight.shape
    bf16, f32 = jnp.bfloat16, jnp.float32
    return pl.pallas_call(
        train_kernel,
        out_shape=[jax.ShapeDtypeStruct((PAIRS, 2, CHUNK, channels), bf16)] * 2,
        in_specs=[SMEM] * 4 + [HBM] * 3 + [VMEM] * 5 + [HBM, VMEM, HBM],
        out_specs=[HBM, HBM],
        scratch_shapes=[
            pltpu.VMEM(packed.shape, bf16),
            pltpu.VMEM((7, 7, channels), f32),
            pltpu.VMEM((2, SLOTS * BAND_TOK, channels), bf16),
            pltpu.VMEM((BAND_TOK, channels), f32),
            pltpu.VMEM((hidden, channels), bf16),
            pltpu.VMEM((hidden, channels), bf16),
            pltpu.VMEM((2, hidden, channels), f32),
            pltpu.VMEM((hidden, 128), f32),
            pltpu.VMEM((hidden, 128), f32),
            pltpu.VMEM((2, PAIRS, 2, CHUNK, channels), bf16),
            pltpu.SMEM((SLOTS + 1,), jnp.int32),
            pltpu.SemaphoreType.DMA((SLOTS - KEPT,)),
            pltpu.SemaphoreType.DMA((SLOTS,)),
            pltpu.SemaphoreType.DMA((2, 2, PAIRS)),
            pltpu.SemaphoreType.DMA((2, PAIRS)),
        ],
        compiler_params=params(56),
        cost_estimate=pl.CostEstimate(flops=9 * 10**9, bytes_accessed=10**7, transcendentals=0),
        name="train",
    )(
        slots, there, count_there, core, *acts, packed, *conv_weights, scale, expand_weight,
        expand_bias, project_weight,
    )


def deal_kernel(got_ref, out):
    total = got_ref[0].astype(jnp.float32)
    for source in range(1, PAIRS):
        total = total + got_ref[source].astype(jnp.float32)
    total = total.astype(jnp.bfloat16)
    row = lax.broadcasted_iota(jnp.int32, (PLANE * DEAL, CHUNK), 0)
    source = lax.broadcasted_iota(jnp.int32, (PLANE * DEAL, CHUNK), 1)
    place = row & (DEAL - 1)
    first = (row >> 4) * SHARE
    dealt = None
    for which in range(2):
        here = place - which * SHARE
        pick = (source == first + here) & (here >= 0) & (here < SHARE)
        part = lax.dot_general(
            jnp.where(pick, 1.0, 0.0).astype(jnp.bfloat16),
            total[which],
            PLAIN,
            preferred_element_type=jnp.float32,
        )
        dealt = part if dealt is None else dealt + part
    out[...] = dealt.astype(jnp.bfloat16).reshape(out.shape)


def deal(got):
    channels = got.shape[-1]
    return pl.pallas_call(
        deal_kernel,
        out_shape=jax.ShapeDtypeStruct((PLANE, DEAL, channels), jnp.bfloat16),
        in_specs=[VMEM],
        out_specs=VMEM,
        compiler_params=params(8),
        name="deal",
    )(got)


def last_kernel(got_ref, in_ref, out_ref):
    total = got_ref[0].astype(jnp.float32)
    for source in range(1, PLANE):
        total = total + got_ref[source].astype(jnp.float32)
    in_ref[...] = total[:SHARE]
    out_ref[...] = total[SHARE : 2 * SHARE]


def last(got):
    share = jax.ShapeDtypeStruct((SHARE, got.shape[-1]), jnp.float32)
    return pl.pallas_call(
        last_kernel,
        out_shape=[share, share],
        in_specs=[VMEM],
        out_specs=[VMEM, VMEM],
        compiler_params=params(4),
        name="last",
    )(got)


def over_chips(a):
    cores = [[place + core for place in range(0, SLOTS, 2)] for core in range(2)]
    return lax.all_to_all(a, "slide", 0, 0, tiled=True, axis_index_groups=cores)


def per_device(
    tile_images,
    cotangent,
    depth_kernel,
    depth_bias,
    norm_gain,
    norm_bias,
    expand_weight,
    expand_bias,
    project_weight,
    layer_scale,
    tile_counts,
    send_list,
):
    slide = lax.axis_index("slide").astype(jnp.int32)
    core = (slide & 1).reshape(1)
    slots = send_list.reshape(-1)
    count = tile_counts.reshape(-1)
    conv_weights = (depth_kernel, depth_bias, norm_gain, norm_bias)
    swap = [(i, i ^ 1) for i in range(16)]
    there = lax.ppermute(slots, "slide", swap)
    count_there = lax.ppermute(count, "slide", swap)
    packed, first = conv_first(
        slots, count, tile_images, cotangent, conv_weights, layer_scale
    )
    packed = lax.ppermute(packed, "slide", swap)
    other = conv_other(slots, count, tile_images, cotangent, conv_weights, layer_scale)
    keep, send = train(
        slots, there, count_there, core, (first, other), packed, conv_weights, layer_scale,
        expand_weight, expand_bias, project_weight,
    )
    got = lax.ppermute(send, "slide", swap)
    both = (keep.astype(jnp.float32) + got.astype(jnp.float32)).astype(jnp.bfloat16)
    got = deal(over_chips(both))
    return tuple(last(lax.all_to_all(got, "rep", 0, 0, tiled=True)))


def solution(mesh):
    in_specs = (
        P(("slide", "rep"), None, None, None),
        P(("slide", "rep"), None, None, None),
        P(),
        P(),
        P(),
        P(),
        P(),
        P(),
        P(),
        P(),
        P("slide", "rep"),
        P("slide", "rep", None),
    )
    out_specs = (P(("slide", "rep"), None), P(("slide", "rep"), None))
    return jax.shard_map(
        per_device, mesh=mesh, in_specs=in_specs, out_specs=out_specs, check_vma=False
    )
```

```python
import jax
import jax.numpy as jnp
from jax import lax
from jax.experimental import pallas as pl
from jax.experimental.pallas import tpu as pltpu
from jax.sharding import PartitionSpec as P

BANDS = 8
MARGIN = 3
BAND_ROWS = 4
BAND_TOK = 128
SLOTS = 16
GROUP = 2
KEPT = 9
FIRST = 2
ROWS = BAND_ROWS + 2 * MARGIN
HID_STEP = 1536
SPAN = GROUP * BAND_TOK
GROUPS = SLOTS // GROUP
PAIRS = 8
CHUNK = 96
PLANE = 16
SHARE = 6
DEAL = 16
JOIN_STEPS = 4

root_half = 0.7071067811865476
inv_root_tau = 0.3989422804014327

INNER = (((1,), (1,)), ((), ()))
PLAIN = (((1,), (0,)), ((), ()))


def half_copies(weight_hbm, weight, core, sems):
    copies = []
    for half in range(2):
        for pair in range(PAIRS):
            first = pl.multiple_of((2 * pair + (core ^ half)) * CHUNK, CHUNK)
            copies.append(
                pltpu.make_async_copy(
                    weight_hbm.at[pl.ds(first, CHUNK)],
                    weight.at[pl.ds((half * PAIRS + pair) * CHUNK, CHUNK)],
                    sems.at[half, pair],
                )
            )
    return copies


def pack_list(slots_ref, order_ref):
    listed = jnp.int32(0)
    for slot in range(SLOTS):
        block = slots_ref[slot]
        order_ref[listed] = jnp.maximum(block, 0)
        listed = listed + jnp.where(block >= 0, 1, 0)
    return listed


def block_copies(order_ref, index, images_hbm, cotan_hbm, images, cotans, sems):
    block = order_ref[index]
    tile = block // BANDS
    band = block % BANDS
    first = band * BAND_ROWS
    above = pltpu.make_async_copy(
        images_hbm.at[tile, pl.ds(first - MARGIN, MARGIN)], images.at[pl.ds(0, MARGIN)], sems.at[0]
    )
    middle = pltpu.make_async_copy(
        images_hbm.at[tile, pl.ds(first, BAND_ROWS)], images.at[pl.ds(MARGIN, BAND_ROWS)], sems.at[1]
    )
    below = pltpu.make_async_copy(
        images_hbm.at[tile, pl.ds(first + BAND_ROWS, MARGIN)],
        images.at[pl.ds(MARGIN + BAND_ROWS, MARGIN)],
        sems.at[2],
    )
    error = pltpu.make_async_copy(cotan_hbm.at[tile, pl.ds(first, BAND_ROWS)], cotans, sems.at[3])
    return band, above, middle, below, error


def start_block(band, above, middle, below, error):
    pl.when(band > 0)(above.start)
    middle.start()
    pl.when(band < BANDS - 1)(below.start)
    error.start()


def conv_norm(image, band, taps, conv_out, depth_bias, gain, norm_bias):
    _, side, channels = image.shape

    @pl.when(band == 0)
    def _():
        image[:MARGIN] = jnp.zeros((MARGIN, side, channels), image.dtype)

    @pl.when(band == BANDS - 1)
    def _():
        image[MARGIN + BAND_ROWS : ROWS] = jnp.zeros((MARGIN, side, channels), image.dtype)

    column = lax.broadcasted_iota(jnp.int32, (8, 128), 0)
    for lanes in range(0, channels, 128):
        part = slice(lanes, lanes + 128)
        flat = image[:, :, part].astype(jnp.float32)
        for row in range(BAND_ROWS):
            sums = [None] * 7
            for dy in range(7):
                x = flat[row + dy]
                for dx in range(7):
                    term = x * taps[dy, dx : dx + 1, part]
                    sums[dx] = term if sums[dx] is None else sums[dx] + term
            total = sums[MARGIN] + depth_bias[:, part]
            for dx in range(-MARGIN, MARGIN + 1):
                if dx != 0:
                    moved = pltpu.roll(sums[dx + MARGIN], (-dx) % side, 0)
                    if dx < 0:
                        edge = jnp.where(column + dx >= 0, moved[:8], 0.0)
                        moved = jnp.concatenate([edge, moved[8:]], axis=0)
                    else:
                        edge = jnp.where(column + dx < 8, moved[side - 8 :], 0.0)
                        moved = jnp.concatenate([moved[: side - 8], edge], axis=0)
                    total = total + moved
            conv_out[row * side : (row + 1) * side, part] = total
    mixed = conv_out[...]
    centre = jnp.mean(mixed, axis=-1, keepdims=True)
    away = mixed - centre
    spread = jnp.mean(away * away, axis=-1, keepdims=True)
    return (away * lax.rsqrt(spread + 1e-06) * gain + norm_bias).astype(jnp.bfloat16)


def scale_errors(errors, scale):
    rows, side, channels = errors.shape
    flat = errors[...].reshape(rows * side, channels)
    return (flat.astype(jnp.float32) * scale).astype(jnp.bfloat16)


def conv_blocks(low, high, refs, between):
    (
        count_ref,
        images_hbm,
        cotan_hbm,
        taps_ref,
        depth_bias_ref,
        gain_ref,
        norm_bias_ref,
        scale_ref,
        acts_hbm,
        images,
        cotans,
        taps,
        acts,
        conv_out,
        order_ref,
        image_sems,
        acts_sems,
    ) = refs
    channels = images_hbm.shape[3]

    def copies(index):
        return block_copies(
            order_ref,
            index,
            images_hbm,
            cotan_hbm,
            images.at[index - low],
            cotans.at[index - low],
            image_sems.at[index - low],
        )

    @pl.loop(low, high)
    def _(index):
        start_block(*copies(index))

    taps[...] = taps_ref[...].astype(jnp.float32)
    depth_bias = depth_bias_ref[...].reshape(1, channels)
    gain = gain_ref[...].reshape(1, channels)
    norm_bias = norm_bias_ref[...].reshape(1, channels)
    scale = scale_ref[...].reshape(1, channels) / count_ref[0].astype(jnp.float32)

    def acts_copy(index):
        rows = pl.ds(pl.multiple_of((index - low) * BAND_TOK, BAND_TOK), BAND_TOK)
        return pltpu.make_async_copy(
            acts.at[:, rows], acts_hbm.at[:, rows], acts_sems.at[index - low]
        )

    @pl.loop(low, high)
    def _(index):
        band, above, middle, below, error = copies(index)
        pl.when(band > 0)(above.wait)
        middle.wait()
        pl.when(band < BANDS - 1)(below.wait)
        rows = pl.ds(pl.multiple_of((index - low) * BAND_TOK, BAND_TOK), BAND_TOK)
        acts[0, rows, :] = conv_norm(
            images.at[index - low], band, taps, conv_out, depth_bias, gain, norm_bias
        )
        error.wait()
        acts[1, rows, :] = scale_errors(cotans.at[index - low], scale)
        acts_copy(index).start()
        if between is not None:
            pl.when(index == low)(between)

    @pl.loop(low, high)
    def _(index):
        acts_copy(index).wait()


def first_kernel(slots_ref, *refs):
    (packed_hbm, acts_hbm), packed, (sems, out_sems) = refs[8:10], refs[15], refs[19:]
    refs = refs[:8] + (acts_hbm,) + refs[10:15] + refs[16:19]
    images_hbm, cotan_hbm, order_ref = refs[1], refs[2], refs[14]
    listed = pack_list(slots_ref, order_ref)

    def copies(index):
        place = packed.at[index - KEPT]
        return block_copies(
            order_ref,
            index,
            images_hbm,
            cotan_hbm,
            place.at[pl.ds(0, ROWS)],
            place.at[pl.ds(ROWS, BAND_ROWS)],
            sems.at[index - KEPT],
        )

    def out_copy(index):
        place = index - KEPT
        return pltpu.make_async_copy(packed.at[place], packed_hbm.at[place], out_sems.at[place])

    @pl.loop(KEPT, listed)
    def _(index):
        start_block(*copies(index))

    def send_out():
        @pl.loop(KEPT, listed)
        def _(index):
            band, above, middle, below, error = copies(index)
            pl.when(band > 0)(above.wait)
            middle.wait()
            pl.when(band < BANDS - 1)(below.wait)
            error.wait()
            out_copy(index).start()

    conv_blocks(0, jnp.minimum(listed, FIRST), refs, send_out)

    @pl.loop(KEPT, listed)
    def _(index):
        out_copy(index).wait()


def other_kernel(slots_ref, *refs):
    listed = pack_list(slots_ref, refs[14])
    conv_blocks(FIRST, jnp.maximum(jnp.minimum(listed, KEPT), FIRST), refs, None)


def train_kernel(
    slots_ref,
    there_ref,
    count_there_ref,
    core_ref,
    first_hbm,
    other_hbm,
    packed_hbm,
    taps_ref,
    depth_bias_ref,
    gain_ref,
    norm_bias_ref,
    scale_ref,
    expand_hbm,
    expand_bias_ref,
    project_hbm,
    keep_hbm,
    send_hbm,
    packed,
    taps,
    acts,
    conv_out,
    expand,
    project,
    grad,
    bias_all,
    bias_ref,
    out,
    order_ref,
    packed_sems,
    acts_sems,
    weight_sems,
    out_sems,
):
    channels = packed_hbm.shape[3]
    core = core_ref[0]
    listed_there = pack_list(there_ref, order_ref)
    listed = jnp.int32(0)
    for slot in range(SLOTS):
        listed = listed + jnp.where(slots_ref[slot] >= 0, 1, 0)
    own = jnp.minimum(listed, KEPT)
    taken = jnp.maximum(listed_there - KEPT, 0)

    def packed_copy(place):
        return pltpu.make_async_copy(packed_hbm.at[place], packed.at[place], packed_sems.at[place])

    def acts_copy(source, low, index):
        rows = pl.ds(pl.multiple_of((index - low) * BAND_TOK, BAND_TOK), BAND_TOK)
        there = pl.ds(pl.multiple_of(index * BAND_TOK, BAND_TOK), BAND_TOK)
        return pltpu.make_async_copy(source.at[:, rows], acts.at[:, there], acts_sems.at[index])

    @pl.loop(0, taken)
    def _(index):
        packed_copy(index).start()

    weight_copies = half_copies(expand_hbm, expand, core, weight_sems.at[0])
    weight_copies += half_copies(project_hbm, project, core, weight_sems.at[1])
    for copy in weight_copies:
        copy.start()

    early = jnp.minimum(own, FIRST)

    @pl.loop(0, early)
    def _(index):
        acts_copy(first_hbm, 0, index).start()

    @pl.loop(FIRST, own)
    def _(index):
        acts_copy(other_hbm, FIRST, index).start()

    hidden = expand_bias_ref.shape[0]
    for first in range(0, hidden, 128):
        row = expand_bias_ref[pl.ds(first, 128)].reshape(1, 128)
        bias_all[pl.ds(first, 128), :] = jnp.broadcast_to(row, (128, 128)).T
    for half in range(2):
        for pair in range(PAIRS):
            rows = pl.ds(pl.multiple_of((2 * pair + (core ^ half)) * CHUNK, CHUNK), CHUNK)
            bias_ref[pl.ds((half * PAIRS + pair) * CHUNK, CHUNK), :] = bias_all[rows, :]
    taps[...] = taps_ref[...].astype(jnp.float32)
    depth_bias = depth_bias_ref[...].reshape(1, channels)
    gain = gain_ref[...].reshape(1, channels)
    norm_bias = norm_bias_ref[...].reshape(1, channels)
    scale = scale_ref[...].reshape(1, channels) / count_there_ref[0].astype(jnp.float32)
    grad[...] = jnp.zeros(grad.shape, jnp.float32)

    @pl.loop(0, taken)
    def _(index):
        packed_copy(index).wait()
        rows = pl.ds(pl.multiple_of((own + index) * BAND_TOK, BAND_TOK), BAND_TOK)
        band = order_ref[KEPT + index] % BANDS
        acts[0, rows, :] = conv_norm(
            packed.at[index, pl.ds(0, ROWS)], band, taps, conv_out, depth_bias, gain, norm_bias
        )
        acts[1, rows, :] = scale_errors(packed.at[index, pl.ds(ROWS, BAND_ROWS)], scale)

    total = own + taken

    @pl.when(total % GROUP != 0)
    def _():
        rows = pl.ds(pl.multiple_of(total * BAND_TOK, BAND_TOK), BAND_TOK)
        acts[:, rows, :] = jnp.zeros((2, BAND_TOK, channels), acts.dtype)

    for copy in weight_copies:
        copy.wait()

    @pl.loop(0, early)
    def _(index):
        acts_copy(first_hbm, 0, index).wait()

    @pl.loop(FIRST, own)
    def _(index):
        acts_copy(other_hbm, FIRST, index).wait()

    half = hidden // 2

    @pl.loop(0, (total + GROUP - 1) // GROUP)
    def _(group):
        rows = pl.ds(pl.multiple_of(group * SPAN, SPAN), SPAN)
        flat_in = acts[0, rows, :]
        flat_err = acts[1, rows, :]
        for start in range(0, 2 * half, HID_STEP):
            units = slice(start, start + HID_STEP)
            pre_act = lax.dot_general(
                expand[units, :], flat_in, INNER, preferred_element_type=jnp.float32
            )
            back_grad = lax.dot_general(
                project[units, :], flat_err, INNER, preferred_element_type=jnp.float32
            )
            pre_act = pre_act + jnp.concatenate([bias_ref[units, :]] * (SPAN // 128), axis=1)
            share = 0.5 * (1.0 + lax.erf(pre_act * root_half))
            activated = (pre_act * share).astype(jnp.bfloat16)
            bell = jnp.exp(-0.5 * pre_act * pre_act) * inv_root_tau
            slope_term = (back_grad * (share + pre_act * bell)).astype(jnp.bfloat16)
            grad[0, units, :] += lax.dot_general(
                slope_term, flat_in, PLAIN, preferred_element_type=jnp.float32
            )
            grad[1, units, :] += lax.dot_general(
                activated, flat_err, PLAIN, preferred_element_type=jnp.float32
            )

    def out_copy(half, pair):
        return pltpu.make_async_copy(
            out.at[half, pair], (keep_hbm, send_hbm)[half].at[pair], out_sems.at[half, pair]
        )

    for half in (1, 0):
        for pair in range(PAIRS):
            rows = slice((half * PAIRS + pair) * CHUNK, (half * PAIRS + pair + 1) * CHUNK)
            out[half, pair] = grad[:, rows, :].astype(out.dtype)
            out_copy(half, pair).start()
    for half in (1, 0):
        for pair in range(PAIRS):
            out_copy(half, pair).wait()


SMEM = pl.BlockSpec(memory_space=pltpu.SMEM)
VMEM = pl.BlockSpec(memory_space=pltpu.VMEM)
HBM = pl.BlockSpec(memory_space=pl.ANY)


def params(mib):
    return pltpu.CompilerParams(vmem_limit_bytes=mib * 2**20)


def conv_scratch(blocks, side, channels):
    bf16, f32 = jnp.bfloat16, jnp.float32
    return [
        pltpu.VMEM((blocks, ROWS, side, channels), bf16),
        pltpu.VMEM((blocks, BAND_ROWS, side, channels), bf16),
        pltpu.VMEM((7, 7, channels), f32),
        pltpu.VMEM((2, blocks * BAND_TOK, channels), bf16),
        pltpu.VMEM((BAND_TOK, channels), f32),
    ]


def conv_first(slots, count, tile_images, cotangent, conv_weights, scale):
    side, channels = tile_images.shape[1], tile_images.shape[3]
    packed = (SLOTS - KEPT, ROWS + BAND_ROWS, side, channels)
    return pl.pallas_call(
        first_kernel,
        out_shape=(
            jax.ShapeDtypeStruct(packed, jnp.bfloat16),
            jax.ShapeDtypeStruct((2, FIRST * BAND_TOK, channels), jnp.bfloat16),
        ),
        in_specs=[SMEM] * 2 + [HBM] * 2 + [VMEM] * 5,
        out_specs=[HBM] * 2,
        scratch_shapes=conv_scratch(FIRST, side, channels)
        + [
            pltpu.VMEM(packed, jnp.bfloat16),
            pltpu.SMEM((SLOTS + 1,), jnp.int32),
            pltpu.SemaphoreType.DMA((FIRST, 4)),
            pltpu.SemaphoreType.DMA((FIRST,)),
            pltpu.SemaphoreType.DMA((SLOTS - KEPT, 4)),
            pltpu.SemaphoreType.DMA((SLOTS - KEPT,)),
        ],
        compiler_params=params(56),
        name="conv_first",
    )(slots, count, tile_images, cotangent, *conv_weights, scale)


def conv_other(slots, count, tile_images, cotangent, conv_weights, scale):
    side, channels = tile_images.shape[1], tile_images.shape[3]
    blocks = KEPT - FIRST
    return pl.pallas_call(
        other_kernel,
        out_shape=jax.ShapeDtypeStruct((2, blocks * BAND_TOK, channels), jnp.bfloat16),
        in_specs=[SMEM] * 2 + [HBM] * 2 + [VMEM] * 5,
        out_specs=HBM,
        scratch_shapes=conv_scratch(blocks, side, channels)
        + [
            pltpu.SMEM((SLOTS + 1,), jnp.int32),
            pltpu.SemaphoreType.DMA((blocks, 4)),
            pltpu.SemaphoreType.DMA((blocks,)),
        ],
        compiler_params=params(62),
        cost_estimate=pl.CostEstimate(flops=8 * 10**9, bytes_accessed=10**7, transcendentals=0),
        name="conv_other",
    )(slots, count, tile_images, cotangent, *conv_weights, scale)


def train(
    slots, there, count_there, core, acts, packed, conv_weights, scale, expand_weight, expand_bias,
    project_weight,
):
    hidden, channels = expand_weight.shape
    bf16, f32 = jnp.bfloat16, jnp.float32
    return pl.pallas_call(
        train_kernel,
        out_shape=[jax.ShapeDtypeStruct((PAIRS, 2, CHUNK, channels), bf16)] * 2,
        in_specs=[SMEM] * 4 + [HBM] * 3 + [VMEM] * 5 + [HBM, VMEM, HBM],
        out_specs=[HBM, HBM],
        scratch_shapes=[
            pltpu.VMEM(packed.shape, bf16),
            pltpu.VMEM((7, 7, channels), f32),
            pltpu.VMEM((2, SLOTS * BAND_TOK, channels), bf16),
            pltpu.VMEM((BAND_TOK, channels), f32),
            pltpu.VMEM((hidden, channels), bf16),
            pltpu.VMEM((hidden, channels), bf16),
            pltpu.VMEM((2, hidden, channels), f32),
            pltpu.VMEM((hidden, 128), f32),
            pltpu.VMEM((hidden, 128), f32),
            pltpu.VMEM((2, PAIRS, 2, CHUNK, channels), bf16),
            pltpu.SMEM((SLOTS + 1,), jnp.int32),
            pltpu.SemaphoreType.DMA((SLOTS - KEPT,)),
            pltpu.SemaphoreType.DMA((SLOTS,)),
            pltpu.SemaphoreType.DMA((2, 2, PAIRS)),
            pltpu.SemaphoreType.DMA((2, PAIRS)),
        ],
        compiler_params=params(56),
        cost_estimate=pl.CostEstimate(flops=9 * 10**9, bytes_accessed=10**7, transcendentals=0),
        name="train",
    )(
        slots, there, count_there, core, *acts, packed, *conv_weights, scale, expand_weight,
        expand_bias, project_weight,
    )


def join_kernel(keep_ref, got_ref, out_ref):
    total = keep_ref[...].astype(jnp.float32) + got_ref[...].astype(jnp.float32)
    out_ref[...] = total.astype(out_ref.dtype)


def join(keep, got):
    part = pl.BlockSpec((PAIRS // JOIN_STEPS,) + keep.shape[1:], lambda step: (step, 0, 0, 0))
    return pl.pallas_call(
        join_kernel,
        out_shape=jax.ShapeDtypeStruct(keep.shape, keep.dtype),
        grid=(JOIN_STEPS,),
        in_specs=[part, part],
        out_specs=part,
        compiler_params=params(8),
        name="join",
    )(keep, got)


def deal_kernel(got_ref, out):
    total = got_ref[0].astype(jnp.float32)
    for source in range(1, PAIRS):
        total = total + got_ref[source].astype(jnp.float32)
    total = total.astype(jnp.bfloat16)
    row = lax.broadcasted_iota(jnp.int32, (PLANE * DEAL, CHUNK), 0)
    source = lax.broadcasted_iota(jnp.int32, (PLANE * DEAL, CHUNK), 1)
    place = row & (DEAL - 1)
    first = (row >> 4) * SHARE
    dealt = None
    for which in range(2):
        here = place - which * SHARE
        pick = (source == first + here) & (here >= 0) & (here < SHARE)
        part = lax.dot_general(
            jnp.where(pick, 1.0, 0.0).astype(jnp.bfloat16),
            total[which],
            PLAIN,
            preferred_element_type=jnp.float32,
        )
        dealt = part if dealt is None else dealt + part
    out[...] = dealt.astype(jnp.bfloat16).reshape(out.shape)


def deal(got):
    channels = got.shape[-1]
    return pl.pallas_call(
        deal_kernel,
        out_shape=jax.ShapeDtypeStruct((PLANE, DEAL, channels), jnp.bfloat16),
        in_specs=[VMEM],
        out_specs=VMEM,
        compiler_params=params(8),
        name="deal",
    )(got)


def last_kernel(got_ref, in_ref, out_ref):
    total = got_ref[0].astype(jnp.float32)
    for source in range(1, PLANE):
        total = total + got_ref[source].astype(jnp.float32)
    in_ref[...] = total[:SHARE]
    out_ref[...] = total[SHARE : 2 * SHARE]


def last(got):
    share = jax.ShapeDtypeStruct((SHARE, got.shape[-1]), jnp.float32)
    return pl.pallas_call(
        last_kernel,
        out_shape=[share, share],
        in_specs=[VMEM],
        out_specs=[VMEM, VMEM],
        compiler_params=params(4),
        name="last",
    )(got)


def over_chips(a):
    cores = [[place + core for place in range(0, SLOTS, 2)] for core in range(2)]
    return lax.all_to_all(a, "slide", 0, 0, tiled=True, axis_index_groups=cores)


def per_device(
    tile_images,
    cotangent,
    depth_kernel,
    depth_bias,
    norm_gain,
    norm_bias,
    expand_weight,
    expand_bias,
    project_weight,
    layer_scale,
    tile_counts,
    send_list,
):
    slide = lax.axis_index("slide").astype(jnp.int32)
    core = (slide & 1).reshape(1)
    slots = send_list.reshape(-1)
    count = tile_counts.reshape(-1)
    conv_weights = (depth_kernel, depth_bias, norm_gain, norm_bias)
    swap = [(i, i ^ 1) for i in range(16)]
    there = lax.ppermute(slots, "slide", swap)
    count_there = lax.ppermute(count, "slide", swap)
    packed, first = conv_first(
        slots, count, tile_images, cotangent, conv_weights, layer_scale
    )
    packed = lax.ppermute(packed, "slide", swap)
    other = conv_other(slots, count, tile_images, cotangent, conv_weights, layer_scale)
    keep, send = train(
        slots, there, count_there, core, (first, other), packed, conv_weights, layer_scale,
        expand_weight, expand_bias, project_weight,
    )
    got = lax.ppermute(send, "slide", swap)
    got = deal(over_chips(join(keep, got)))
    return tuple(last(lax.all_to_all(got, "rep", 0, 0, tiled=True)))


def solution(mesh):
    in_specs = (
        P(("slide", "rep"), None, None, None),
        P(("slide", "rep"), None, None, None),
        P(),
        P(),
        P(),
        P(),
        P(),
        P(),
        P(),
        P(),
        P("slide", "rep"),
        P("slide", "rep", None),
    )
    out_specs = (P(("slide", "rep"), None), P(("slide", "rep"), None))
    return jax.shard_map(
        per_device, mesh=mesh, in_specs=in_specs, out_specs=out_specs, check_vma=False
    )
```
